32 devices in a mesh: prompt: 4 (over x, core), resp: 8 (over z, y).
Axes of the slice: x: 2, y: 2, z: 4, core: 2. Of those that a mesh axis runs over, the one named last changes fastest.
Arguments:
- queries: bfloat16 [4, 1024, 8192], P('prompt', 'resp'), may hold values from -6 to 6
- resp_kv: bfloat16 [4, 1024, 2048], P('prompt', 'resp'), may hold values from -6 to 6
- resp_segments: int32 [4, 1024], P('prompt', 'resp'), may hold values from 0 to 1, never falling along the last dimension, each value on 1 to 896 neighbouring positions
- prefix_kv: bfloat16 [128, 8, 2048], P(('prompt', 'resp')), may hold values from -6 to 6
- tile_plan: int32 [128, 2], P(('prompt', 'resp')), may hold values from 0 to 31, as said below
- prompt_lengths: int32 [4], P('prompt'), may hold values from 8 to 256
Outputs:
- attended: bfloat16 [4, 1024, 8192], P('prompt', 'resp')
The draws below stay inside these ranges and needn't reach their ends.
Inputs may be any that keep to these rules, and one draw needn't show every extreme that they name: `tile_plan`: column 0 is a group in 0 .. 3 and column 1 a place in 0 .. 31; each pair of group and place stands once; the 4 tiles of each device hold one tile of every group, in any order. `resp_segments`: response numbers never fall along a group's tokens; each response has 1 to 896 tokens.
All inputs are finite; a program needn't handle non-finite values.
Results may differ from the reference program's by a relative error of at most 0.0055.
Values may be sent and summed in bfloat16 or wider, within the bound.
No kernel may reach another device: no remote copies, remote signals or barrier semaphores. Data moves between devices by JAX's collectives and lax.ppermute only.
A program may use at most 128 MiB of HBM per device.

```python
import math
import jax
import jax.numpy as jnp
import numpy as np
from jax import lax

H = 64
KVH = 8
HD = 128
ROWS = 128
TILE = 8
TPG = 1
GROUPS = 4
RTOK = 1024
SEGS = 2
TILES = 128
PMAX = 256
N_RESP = 8
DEVICES = 32


def draw_queries(key, part):
    shape = (GROUPS, RTOK, H * HD)
    return jnp.clip(jax.random.normal(jax.random.fold_in(key, 11), shape, jnp.float32), -6.0, 6.0).astype(jnp.bfloat16)


def draw_prefix_kv(key, part):
    shape = (TILES, TILE, 2 * KVH * HD)
    return jnp.clip(jax.random.normal(jax.random.fold_in(key, 13), shape, jnp.float32), -6.0, 6.0).astype(jnp.bfloat16)


def draw_tile_plan(key, part):
    per_group = DEVICES * TPG
    slots = GROUPS * TPG
    places = jnp.stack([jax.random.permutation(jax.random.fold_in(key, 100 + g), per_group) for g in range(GROUPS)])
    places = jnp.transpose(places.reshape(GROUPS, DEVICES, TPG), (1, 0, 2)).reshape(DEVICES, slots)
    owners = jnp.broadcast_to(jnp.repeat(jnp.arange(GROUPS, dtype=jnp.int32), TPG)[None, :], (DEVICES, slots))
    shuffle_keys = jax.random.split(jax.random.fold_in(key, 5), DEVICES)
    shuffles = jax.vmap(lambda one: jax.random.permutation(one, slots))(shuffle_keys)
    owners = jnp.take_along_axis(owners, shuffles, axis=1)
    places = jnp.take_along_axis(places.astype(jnp.int32), shuffles, axis=1)
    return jnp.stack([owners, places], axis=-1).reshape(DEVICES * slots, 2).astype(jnp.int32)


def touch_ends(result, rng, low, high):
    spot = [jax.random.randint(jax.random.fold_in(rng, axis), (), 0, length) for axis, length in enumerate(result.shape)]
    main_axis = result.shape.index(max(result.shape))
    next_to = spot[:main_axis] + [(spot[main_axis] + 1) % result.shape[main_axis]] + spot[main_axis + 1:]
    return result.at[tuple(spot)].set(low).at[tuple(next_to)].set(high)


def steps_of(key, shape, shards, least, largest):
    level = 1.0
    for dim, shards_of in shards:
        heights = jax.random.uniform(jax.random.fold_in(jax.random.fold_in(key, 6), dim), (shards_of,), jnp.float32, least / len(shards), largest / len(shards))
        level = level * jnp.repeat(jnp.exp(heights), shape[dim] // shards_of).reshape((-1,) + (1,) * (len(shape) - 1 - dim))
    return level


def length_profile(count, total, bound, slope):
    portions = [(1 << 20) // math.isqrt(standing ** slope) + 1 for standing in range(2, count + 1)]
    spare, holding = total - bound - (count - 1), [1] * (count - 1)
    while spare > 0:
        free = [i for i in range(count - 1) if holding[i] < bound]
        mass, left = sum([portions[i] for i in free]), spare
        for i in free:
            more = min(bound - holding[i], max(1, left * portions[i] // mass), spare)
            holding[i] = holding[i] + more
            spare = spare - more
    return np.array([bound] + holding)


def uneven(stream_key, number_of, total, most, lean):
    if number_of == 2:
        one = jax.random.randint(stream_key, (), max(1, total - most), min(most, total - 1) + 1)
        return jnp.stack([one, total - one])
    lengths = jnp.asarray(length_profile(number_of, total, most, lean), jnp.int32)
    couples = (number_of - 1) // 2
    source_of, receiver = lengths[1:1 + 2 * couples:2], lengths[2:2 + 2 * couples:2]
    margin = jnp.minimum(source_of - 1, most - receiver)
    passed = jax.random.randint(jax.random.fold_in(stream_key, 1), (couples,), 0, 1 << 20) % (margin + 1)
    lengths = lengths.at[1:1 + 2 * couples:2].set(source_of - passed).at[2:2 + 2 * couples:2].set(receiver + passed)
    return lengths[jax.random.permutation(jax.random.fold_in(stream_key, 2), number_of)]


def bell_draw(key, dims, width, bound, cuts=(), kind=jnp.bfloat16):
    entries = width * jax.random.normal(key, dims, jnp.float32)
    if cuts:
        entries = entries * steps_of(key, dims, cuts, -0.22, 0.18)
    return jnp.clip(entries, -bound, bound).astype(kind)


def setup_inputs(seed: int = 0) -> dict:
    keys = jax.random.split(jax.random.key(seed), 7)
    queries = draw_queries(jax.random.fold_in(keys[6], 71), 0)
    resp_kv = bell_draw(keys[1], (GROUPS, RTOK, 2 * KVH * HD), 1.0, 6.0, ((0, 4), (1, 8)))
    resp_segments = jax.vmap(lambda own: jnp.searchsorted(jnp.cumsum(uneven(own, SEGS, RTOK, 7 * ROWS, 1)), jnp.arange(RTOK), side="right"))(jax.random.split(keys[2], GROUPS)).reshape((GROUPS, RTOK)).astype(jnp.int32)
    prefix_kv = draw_prefix_kv(jax.random.fold_in(keys[6], 71), 0)
    tile_plan = draw_tile_plan(jax.random.fold_in(keys[6], 71), 0)
    prompt_lengths = touch_ends(jax.random.randint(keys[5], (GROUPS,), TILE, PMAX + 1), jax.random.fold_in(keys[5], 1), TILE, PMAX).astype(jnp.int32)
    return {"queries": queries, "resp_kv": resp_kv, "resp_segments": resp_segments, "prefix_kv": prefix_kv, "tile_plan": tile_plan, "prompt_lengths": prompt_lengths}


NEG_FILL = -1.0e30


def reference(queries, resp_kv, resp_segments, prefix_kv, tile_plan, prompt_lengths):
    split = KVH * HD
    group_size = H // KVH
    score_scale = 1.0 / (HD ** 0.5)
    reach = 7
    order = jnp.argsort(tile_plan[:, 0], stable=True)
    tiles = prefix_kv[order]
    plan = tile_plan[order]
    per_group = TILES // GROUPS
    tiles = tiles.reshape(GROUPS, per_group * TILE, 2 * split)
    places = (plan[:, 1][:, None] * TILE + jnp.arange(TILE, dtype=jnp.int32)[None, :]).reshape(GROUPS, per_group * TILE)
    resp_pad = jnp.concatenate([jnp.zeros((GROUPS, reach * ROWS, 2 * split), resp_kv.dtype), resp_kv], axis=1)
    seg_pad = jnp.concatenate([jnp.full((GROUPS, reach * ROWS), -1, jnp.int32), resp_segments.astype(jnp.int32)], axis=1)

    def one_block(index):
        group = (index // N_RESP).astype(jnp.int32)
        block = (index % N_RESP).astype(jnp.int32)
        start = (block * ROWS).astype(jnp.int32)
        zero = jnp.zeros((), jnp.int32)
        query = lax.dynamic_slice(queries, (group, start, zero), (1, ROWS, H * HD))[0]
        near = lax.dynamic_slice(resp_pad, (group, start, zero), (1, (reach + 1) * ROWS, 2 * split))[0]
        near_seg = lax.dynamic_slice(seg_pad, (group, start), (1, (reach + 1) * ROWS))[0]
        own_seg = lax.dynamic_slice(resp_segments.astype(jnp.int32), (group, start), (1, ROWS))[0]
        prefix = lax.dynamic_index_in_dim(tiles, group, 0, keepdims=False)
        prefix_live = lax.dynamic_index_in_dim(places, group, 0, keepdims=False) < lax.dynamic_index_in_dim(prompt_lengths, group, 0, keepdims=False)
        key_vectors = jnp.concatenate([prefix[:, :split], near[:, :split]], axis=0).reshape(-1, KVH, HD)
        value_vectors = jnp.concatenate([prefix[:, split:], near[:, split:]], axis=0).reshape(-1, KVH, HD)
        query_pos = jnp.arange(ROWS, dtype=jnp.int32)
        key_pos = jnp.arange((reach + 1) * ROWS, dtype=jnp.int32) - reach * ROWS
        resp_visible = (near_seg[None, :] == own_seg[:, None]) & (key_pos[None, :] <= query_pos[:, None])
        visible = jnp.concatenate([jnp.broadcast_to(prefix_live[None, :], (ROWS, prefix.shape[0])), resp_visible], axis=1)
        query_head_rows = query.reshape(ROWS, KVH, group_size, HD).astype(jnp.float32)
        logit_scores = jnp.einsum("wcpo,lco->wcpl", query_head_rows, key_vectors.astype(jnp.float32)) * score_scale
        mask = visible[:, None, None, :]
        logit_scores = jnp.where(mask, logit_scores, NEG_FILL)
        top = jnp.max(logit_scores, axis=-1, keepdims=True)
        attention_weight = jnp.where(mask, jnp.exp(logit_scores - top), 0.0)
        total = jnp.sum(attention_weight, axis=-1)
        rounded_probs = lax.optimization_barrier(attention_weight.astype(jnp.bfloat16)).astype(jnp.float32)
        weighted_sum = jnp.einsum("luem,mut->luet", rounded_probs, value_vectors.astype(jnp.float32))
        return (weighted_sum / total[..., None]).reshape(ROWS, H * HD).astype(jnp.bfloat16)

    blocks = lax.map(one_block, jnp.arange(GROUPS * N_RESP, dtype=jnp.int32))
    return blocks.reshape(GROUPS, RTOK, H * HD)
```

```python
import functools
import math

import jax
import jax.numpy as jnp
from jax import lax
from jax.experimental import pallas as pl
from jax.experimental.pallas import tpu as pltpu
from jax.sharding import PartitionSpec as P

H = 64
KVH = 8
HD = 128
GQ = H // KVH
REACH = 7
STEP = 256
FILL = -1e30
CHUNKS = (2, 2, 2, 2)


def attend_kernel(
    meta_ref, seg_q_ref, seg_k_ref, prefix_bias_ref, q_ref, k_ref, v_ref, pk_ref, pv_ref, *rest
):
    o_ref, s_ref, top_ref, acc_ref, bias_ref = rest[-5:]
    rows = q_ref.shape[0]
    prefix_steps = pk_ref.shape[0] // STEP
    first, last, row0 = meta_ref[0], meta_ref[1], meta_ref[2]
    scale = math.log2(math.e) / math.sqrt(HD)
    nt = (((1,), (1,)), ((), ()))

    @pl.when(pl.program_id(0) == 0)
    def _():
        def fill(step, _):
            start = pl.multiple_of(step * STEP, STEP)
            seg_k = seg_k_ref[:, pl.ds(start, STEP)]
            key_pos = start + lax.broadcasted_iota(jnp.int32, (rows, STEP), 1)
            row_pos = row0 + lax.broadcasted_iota(jnp.int32, (rows, STEP), 0)
            seen = (seg_k == seg_q_ref[...]) & (key_pos <= row_pos)
            bias_ref[step - first] = jnp.where(seen, 0.0, FILL)
            return 0

        lax.fori_loop(first, last + 1, fill, 0)

    q = jnp.concatenate([q_ref[:, g * HD : (g + 1) * HD] for g in range(GQ)], axis=0)

    def scores(keys, bias, slot, fresh):
        s = lax.dot_general(q, keys, nt, preferred_element_type=jnp.float32)
        s = (s.reshape(GQ, -1, STEP) + bias[None]).reshape(-1, STEP)
        s_ref[slot] = s
        top = jnp.maximum(s[:, :HD], s[:, HD:])
        top_ref[...] = top if fresh else jnp.maximum(top_ref[...], top)

    for step in range(prefix_steps):
        at = pl.ds(step * STEP, STEP)
        scores(pk_ref[at, :], prefix_bias_ref[:, at], step, step == 0)

    def score_step(step, _):
        at = pl.ds(pl.multiple_of(step * STEP, STEP), STEP)
        scores(k_ref[at, :], bias_ref[step - first], prefix_steps + step - first, False)
        return 0

    lax.fori_loop(first, last + 1, score_step, 0)
    top = jnp.max(top_ref[...], axis=1, keepdims=True)
    top_ref[...] = jnp.broadcast_to(top, top_ref.shape)
    ones = jnp.ones((STEP, HD), jnp.bfloat16)

    def weigh(values, slot, fresh):
        both = jnp.concatenate([values, ones], axis=1)
        for g in range(GQ):
            at = pl.ds(g * rows, rows)
            s = s_ref[slot, at, :]
            t = top_ref[at, :]
            w = jnp.concatenate(
                [jnp.exp2((s[:, :HD] - t) * scale), jnp.exp2((s[:, HD:] - t) * scale)], axis=1
            )
            add = jnp.dot(w.astype(jnp.bfloat16), both, preferred_element_type=jnp.float32)
            acc_ref[at, :] = add if fresh else acc_ref[at, :] + add

    for step in range(prefix_steps):
        weigh(pv_ref[pl.ds(step * STEP, STEP), :], step, step == 0)

    def weigh_step(step, _):
        at = pl.ds(pl.multiple_of(step * STEP, STEP), STEP)
        weigh(v_ref[at, :], prefix_steps + step - first, False)
        return 0

    lax.fori_loop(first, last + 1, weigh_step, 0)
    for g in range(GQ):
        at = pl.ds(g * rows, rows)
        o_ref[:, g * HD : (g + 1) * HD] = (acc_ref[at, :HD] / acc_ref[at, HD:]).astype(o_ref.dtype)


def attend(meta, seg_q, seg_k, prefix_bias, queries, kv, prefix, out, head0, heads):
    rows = queries.shape[0]
    keys, prefix_keys = kv.shape[0], prefix.shape[0]
    slots = min(-(-keys // STEP), REACH * rows // STEP + 2)
    wide = (rows, GQ * HD)
    in_specs = [
        pl.BlockSpec((rows, 1), lambda i, m: (0, 0)),
        pl.BlockSpec((1, keys), lambda i, m: (0, 0)),
        pl.BlockSpec((1, prefix_keys), lambda i, m: (0, 0)),
        pl.BlockSpec(wide, lambda i, m: (0, head0 + i)),
        pl.BlockSpec((keys, HD), lambda i, m: (0, i)),
        pl.BlockSpec((keys, HD), lambda i, m: (0, heads + i)),
        pl.BlockSpec((prefix_keys, HD), lambda i, m: (0, head0 + i)),
        pl.BlockSpec((prefix_keys, HD), lambda i, m: (0, KVH + head0 + i)),
    ]
    args = [meta, seg_q, seg_k, prefix_bias, queries, kv, kv, prefix, prefix]
    aliases = {}
    if out is not None:
        in_specs.append(pl.BlockSpec(memory_space=pl.ANY))
        args.append(out)
        aliases = {len(args) - 1: 0}
    return pl.pallas_call(
        attend_kernel,
        grid_spec=pltpu.PrefetchScalarGridSpec(
            num_scalar_prefetch=1,
            grid=(heads,),
            in_specs=in_specs,
            out_specs=pl.BlockSpec(wide, lambda i, m: (0, head0 + i)),
            scratch_shapes=[
                pltpu.VMEM((slots + prefix_keys // STEP, GQ * rows, STEP), jnp.float32),
                pltpu.VMEM((GQ * rows, HD), jnp.float32),
                pltpu.VMEM((GQ * rows, 2 * HD), jnp.float32),
                pltpu.VMEM((slots, rows, STEP), jnp.float32),
            ],
        ),
        out_shape=jax.ShapeDtypeStruct(queries.shape, queries.dtype),
        input_output_aliases=aliases,
        compiler_params=pltpu.CompilerParams(vmem_limit_bytes=40 * 1024 * 1024),
    )(*args)


def on_device(queries, resp_kv, resp_segments, prefix_kv, tile_plan, prompt_lengths):
    rows = queries.shape[1]
    split = KVH * HD
    tiles, tile = prefix_kv.shape[:2]
    groups = lax.axis_size("prompt")
    per = tiles // groups
    group = lax.axis_index("prompt")
    block = lax.axis_index("resp")

    owner, place = tile_plan[:, 0], tile_plan[:, 1]
    index = jnp.arange(tiles, dtype=jnp.int32)
    ahead = (owner[None, :] < owner[:, None]) | (
        (owner[None, :] == owner[:, None]) & (index[None, :] < index[:, None])
    )
    rank = jnp.sum(ahead, axis=1, dtype=jnp.int32)
    pick = rank[None, :] == index[:, None]
    sorted_place = jnp.sum(jnp.where(pick, place[None, :], 0), axis=1, dtype=jnp.int32)
    sorted_tiles = jnp.sum(
        jnp.where(pick[:, :, None, None], prefix_kv[None], 0).astype(jnp.float32), axis=1
    ).astype(prefix_kv.dtype)

    ints = jnp.concatenate([resp_segments[0], sorted_place])
    ints = lax.all_gather(ints, ("prompt", "resp"), axis=0, tiled=False)
    ints = ints.reshape(groups, -1, rows + tiles)

    pieces = []
    head = 0
    for heads in CHUNKS:
        k = resp_kv[0, :, head * HD : (head + heads) * HD]
        v = resp_kv[0, :, split + head * HD : split + (head + heads) * HD]
        piece = jnp.concatenate([k, v], axis=1)
        pieces.append((head, heads, lax.all_gather(piece, "resp", axis=0, tiled=True)))
        head += heads
    moved = lax.all_to_all(sorted_tiles, "prompt", split_axis=0, concat_axis=0, tiled=True)
    prefix = lax.all_gather(moved, "resp", axis=0, tiled=True).reshape(-1, 2 * split)

    seg_k = lax.dynamic_index_in_dim(ints, group, 0, keepdims=False)[:, :rows].reshape(1, -1)
    places = lax.dynamic_slice_in_dim(ints, rows + group * per, per, 2)
    places = jnp.transpose(places, (1, 0, 2)).reshape(-1, 1)
    places = places * tile + jnp.arange(tile, dtype=jnp.int32)[None, :]
    prefix_bias = jnp.where(places < prompt_lengths[0], 0.0, FILL).reshape(1, -1)
    seg_q = resp_segments[0][:, None]
    before = jnp.sum(seg_k < resp_segments[0, 0], dtype=jnp.int32)
    row0 = block * rows
    meta = jnp.stack([before // STEP, row0 // STEP, row0])

    out = None
    for head, heads, kv in pieces:
        out = attend(meta, seg_q, seg_k, prefix_bias, queries[0], kv, prefix, out, head, heads)
    return out[None]


def solution(mesh):
    return jax.shard_map(
        on_device,
        mesh=mesh,
        in_specs=(
            P("prompt", "resp", None),
            P("prompt", "resp", None),
            P("prompt", "resp"),
            P(("prompt", "resp"), None, None),
            P(("prompt", "resp"), None),
            P("prompt"),
        ),
        out_specs=P("prompt", "resp", None),
        check_vma=False,
    )
```

```python
import functools
import math

import jax
import jax.numpy as jnp
from jax import lax
from jax.experimental import pallas as pl
from jax.experimental.pallas import tpu as pltpu
from jax.sharding import PartitionSpec as P

H = 64
KVH = 8
HD = 128
GQ = H // KVH
REACH = 7
STEP = 256
FILL = -1e30
CHUNKS = 1


def attend_kernel(pairs, meta_ref, seg_q_ref, seg_k_ref, prefix_bias_ref, q_ref, pk_ref, pv_ref, *rest):
    k_refs, v_refs = rest[:pairs], rest[pairs : 2 * pairs]
    o_ref, s_ref, top_ref, acc_ref, bias_ref = rest[-5:]
    rows = q_ref.shape[0]
    span = k_refs[0].shape[0]
    prefix_steps = pk_ref.shape[0] // STEP
    own_pair, reach, row0 = meta_ref[0], meta_ref[1], meta_ref[2]
    scale = math.log2(math.e) / math.sqrt(HD)
    nt = (((1,), (1,)), ((), ()))

    def each_pair(body):
        for k in range(pairs):
            pl.when(k <= reach)(functools.partial(body, k))

    @pl.when(pl.program_id(0) == 0)
    def _():
        def fill(k):
            start = pl.multiple_of((own_pair - k) * span, span)
            seg_k = seg_k_ref[:, pl.ds(start, span)]
            key_pos = start + lax.broadcasted_iota(jnp.int32, (rows, span), 1)
            row_pos = row0 + lax.broadcasted_iota(jnp.int32, (rows, span), 0)
            seen = (seg_k == seg_q_ref[...]) & (key_pos <= row_pos)
            bias_ref[k] = jnp.where(seen, 0.0, FILL)

        each_pair(fill)

    q = jnp.concatenate([q_ref[:, g * HD : (g + 1) * HD] for g in range(GQ)], axis=0)

    def scores(keys, bias, slot, fresh):
        s = lax.dot_general(q, keys, nt, preferred_element_type=jnp.float32)
        s = (s.reshape(GQ, rows, -1) + bias[None]).reshape(GQ * rows, -1)
        s_ref[slot] = s
        top = jnp.maximum(s[:, :HD], s[:, HD:])
        top_ref[...] = top if fresh else jnp.maximum(top_ref[...], top)

    for step in range(prefix_steps):
        at = pl.ds(step * STEP, STEP)
        scores(pk_ref[at, :], prefix_bias_ref[:, at], step, step == 0)
    each_pair(lambda k: scores(k_refs[k][...], bias_ref[k], prefix_steps + k, False))

    top = jnp.max(top_ref[...], axis=1, keepdims=True)
    top_ref[...] = jnp.broadcast_to(top, top_ref.shape)

    def weigh(values, slot, fresh):
        both = jnp.concatenate([values, jnp.ones((values.shape[0], HD), values.dtype)], axis=1)
        for g in range(GQ):
            at = pl.ds(g * rows, rows)
            s = s_ref[slot, at, :]
            t = top_ref[at, :]
            w = jnp.concatenate(
                [jnp.exp2((s[:, :HD] - t) * scale), jnp.exp2((s[:, HD:] - t) * scale)], axis=1
            )
            add = jnp.dot(w.astype(jnp.bfloat16), both, preferred_element_type=jnp.float32)
            acc_ref[at, :] = add if fresh else acc_ref[at, :] + add

    for step in range(prefix_steps):
        weigh(pv_ref[pl.ds(step * STEP, STEP), :], step, step == 0)
    each_pair(lambda k: weigh(v_refs[k][...], prefix_steps + k, False))
    for g in range(GQ):
        at = pl.ds(g * rows, rows)
        o_ref[:, g * HD : (g + 1) * HD] = (acc_ref[at, :HD] / acc_ref[at, HD:]).astype(o_ref.dtype)


def attend(meta, seg_q, seg_k, prefix_bias, queries, pieces, prefix, out):
    rows = queries.shape[0]
    prefix_keys = prefix.shape[0]
    pairs, span = len(pieces), pieces[0].shape[0]
    heads = pieces[0].shape[1] // (2 * HD)
    wide = (rows, GQ * HD)
    in_specs = [
        pl.BlockSpec((rows, 1), lambda i, m: (0, 0)),
        pl.BlockSpec(seg_k.shape, lambda i, m: (0, 0)),
        pl.BlockSpec((1, prefix_keys), lambda i, m: (0, 0)),
        pl.BlockSpec(wide, lambda i, m: (0, m[3] + i)),
        pl.BlockSpec((prefix_keys, HD), lambda i, m: (0, m[3] + i)),
        pl.BlockSpec((prefix_keys, HD), lambda i, m: (0, KVH + m[3] + i)),
        *[pl.BlockSpec((span, HD), lambda i, m: (0, i))] * pairs,
        *[pl.BlockSpec((span, HD), lambda i, m: (0, heads + i))] * pairs,
    ]
    args = [meta, seg_q, seg_k, prefix_bias, queries, prefix, prefix, *pieces, *pieces]
    aliases = {}
    if out is not None:
        in_specs.append(pl.BlockSpec(memory_space=pl.ANY))
        args.append(out)
        aliases = {len(args) - 1: 0}
    return pl.pallas_call(
        functools.partial(attend_kernel, pairs),
        grid_spec=pltpu.PrefetchScalarGridSpec(
            num_scalar_prefetch=1,
            grid=(heads,),
            in_specs=in_specs,
            out_specs=pl.BlockSpec(wide, lambda i, m: (0, m[3] + i)),
            scratch_shapes=[
                pltpu.VMEM((pairs + prefix_keys // STEP, GQ * rows, span), jnp.float32),
                pltpu.VMEM((GQ * rows, HD), jnp.float32),
                pltpu.VMEM((GQ * rows, 2 * HD), jnp.float32),
                pltpu.VMEM((pairs, rows, span), jnp.float32),
            ],
        ),
        out_shape=jax.ShapeDtypeStruct(queries.shape, queries.dtype),
        input_output_aliases=aliases,
        compiler_params=pltpu.CompilerParams(vmem_limit_bytes=40 * 1024 * 1024),
    )(*args)


def on_device(queries, resp_kv, resp_segments, prefix_kv, tile_plan, prompt_lengths):
    rows = queries.shape[1]
    split = KVH * HD
    tiles, tile = prefix_kv.shape[:2]
    groups, count = lax.axis_size("prompt"), lax.axis_size("resp")
    per = tiles // groups
    group = lax.axis_index("prompt")
    block = lax.axis_index("resp")
    side = block % 2
    steps = min(count // 2 - 1, (REACH + 1) // 2)
    heads = KVH // 2 // CHUNKS

    def part(owner, chunk):
        head = (owner * (KVH // 2) + chunk * heads) * HD
        k = lax.dynamic_slice_in_dim(resp_kv[0], head, heads * HD, 1)
        v = lax.dynamic_slice_in_dim(resp_kv[0], split + head, heads * HD, 1)
        return jnp.concatenate([k, v], axis=1)

    def swap(value, first):
        return lax.ppermute(value, "resp", [(r, r ^ 1) for r in range(2 * first, count)])

    def pair_of(own, other):
        return jnp.where(
            side == 0, jnp.concatenate([own, other]), jnp.concatenate([other, own])
        )

    straight, crossed = [], []
    for chunk in range(CHUNKS):
        mine, theirs = part(side, chunk), part(1 - side, chunk)
        straight.append([pair_of(mine, swap(theirs, 0))])
        upper = lax.ppermute(mine, "resp", [(r, r + 1) for r in range(0, count, 2)])
        crossed.append([pair_of(theirs, upper)])
    for step in range(1, steps + 1):
        for chunk in range(CHUNKS):
            moved = lax.ppermute(
                straight[chunk][-1], "resp", [(r, r + 2) for r in range(2 * step - 2, count - 2)]
            )
            straight[chunk].append(moved)
            crossed[chunk].append(swap(moved, step))

    owner, place = tile_plan[:, 0], tile_plan[:, 1]
    index = jnp.arange(tiles, dtype=jnp.int32)
    ahead = (owner[None, :] < owner[:, None]) | (
        (owner[None, :] == owner[:, None]) & (index[None, :] < index[:, None])
    )
    rank = jnp.sum(ahead, axis=1, dtype=jnp.int32)
    pick = rank[None, :] == index[:, None]
    sorted_place = jnp.sum(jnp.where(pick, place[None, :], 0), axis=1, dtype=jnp.int32)
    sorted_tiles = jnp.sum(
        jnp.where(pick[:, :, None, None], prefix_kv[None], 0).astype(jnp.float32), axis=1
    ).astype(prefix_kv.dtype)

    ints = jnp.concatenate([resp_segments[0], sorted_place])
    ints = jnp.broadcast_to(ints[None], (groups * count, rows + tiles))
    ints = lax.all_to_all(ints, ("prompt", "resp"), split_axis=0, concat_axis=0, tiled=True)
    ints = ints.reshape(groups, count, rows + tiles)
    moved = lax.all_to_all(sorted_tiles, "prompt", split_axis=0, concat_axis=0, tiled=True)
    prefix = lax.all_gather(moved, "resp", axis=0, tiled=True).reshape(-1, 2 * split)

    seg_k = lax.dynamic_index_in_dim(ints, group, 0, keepdims=False)[:, :rows].reshape(1, -1)
    places = lax.dynamic_slice_in_dim(ints, rows + group * per, per, 2)
    places = jnp.transpose(places, (1, 0, 2)).reshape(-1, 1)
    places = places * tile + jnp.arange(tile, dtype=jnp.int32)[None, :]
    prefix_bias = jnp.where(places < prompt_lengths[0], 0.0, FILL).reshape(1, -1)
    seg_q = resp_segments[0][:, None]
    before = jnp.sum(seg_k < resp_segments[0, 0], dtype=jnp.int32)
    own_pair = block // 2

    out = None
    for pieces_of, owner_side in ((straight, side), (crossed, 1 - side)):
        for chunk in range(CHUNKS):
            head0 = owner_side * (KVH // 2) + chunk * heads
            meta = jnp.stack([own_pair, own_pair - before // (2 * rows), block * rows, head0])
            out = attend(
                meta, seg_q, seg_k, prefix_bias, queries[0], pieces_of[chunk], prefix, out
            )
    return out[None]


def solution(mesh):
    return jax.shard_map(
        on_device,
        mesh=mesh,
        in_specs=(
            P("prompt", "resp", None),
            P("prompt", "resp", None),
            P("prompt", "resp"),
            P(("prompt", "resp"), None, None),
            P(("prompt", "resp"), None),
            P("prompt"),
        ),
        out_specs=P("prompt", "resp", None),
        check_vma=False,
    )
```

```python
import functools
import math

import jax
import jax.numpy as jnp
from jax import lax
from jax.experimental import pallas as pl
from jax.experimental.pallas import tpu as pltpu
from jax.sharding import PartitionSpec as P

H = 64
KVH = 8
HD = 128
GQ = H // KVH
REACH = 7
SLAB = 2
FILL = -1e30


def attend_kernel(pairs, meta_ref, seg_q_ref, seg_k_ref, prefix_bias_ref, q_ref, pk_ref, pv_ref, *rest):
    k_refs, v_refs = rest[: 2 * pairs], rest[2 * pairs : 4 * pairs]
    o_ref, s_ref, top_ref, bias_ref = rest[-4:]
    rows = q_ref.shape[0]
    step = 2 * rows
    prefix_steps = pk_ref.shape[0] // step
    block, reach = meta_ref[0], meta_ref[1]
    scale = math.log2(math.e) / math.sqrt(HD)
    nt = (((1,), (1,)), ((), ()))

    @pl.when(pl.program_id(0) == 0)
    def _():
        row_pos = block * rows + lax.broadcasted_iota(jnp.int32, (rows, rows), 0)
        lane = lax.broadcasted_iota(jnp.int32, (rows, rows), 1)
        for k in range(pairs):
            for part, first in enumerate((block, block + 1 - 2 * lax.rem(block, 2))):
                key_block = jnp.maximum(first - 2 * k, 0)
                seen = (seg_k_ref[key_block] == seg_q_ref[...]) & (
                    key_block * rows + lane <= row_pos
                )
                bias_ref[k, :, part * rows : (part + 1) * rows] = jnp.where(seen, 0.0, FILL)

    def body(near):
        keys = [pk_ref[i * step : (i + 1) * step, :] for i in range(prefix_steps)]
        values = [pv_ref[i * step : (i + 1) * step, :] for i in range(prefix_steps)]
        for k in range(near + 1):
            keys.append(jnp.concatenate([k_refs[2 * k][...], k_refs[2 * k + 1][...]]))
            values.append(jnp.concatenate([v_refs[2 * k][...], v_refs[2 * k + 1][...]]))
        values = jnp.concatenate(values)
        values = jnp.concatenate([values, jnp.ones_like(values)], axis=1)

        def score(slab):
            heads = range(slab * SLAB, (slab + 1) * SLAB)
            q = jnp.concatenate([q_ref[:, g * HD : (g + 1) * HD] for g in heads])
            top = None
            for i, key in enumerate(keys):
                s = lax.dot_general(q, key, nt, preferred_element_type=jnp.float32)
                if i < prefix_steps:
                    bias = prefix_bias_ref[:, i * step : (i + 1) * step]
                else:
                    bias = bias_ref[i - prefix_steps]
                s = (s.reshape(SLAB, rows, step) + bias[None]).reshape(SLAB * rows, step)
                s_ref[slab % 2, :, i * step : (i + 1) * step] = s
                high = jnp.maximum(s[:, :rows], s[:, rows:])
                top = high if top is None else jnp.maximum(top, high)
            top = jnp.max(top, axis=1, keepdims=True)
            top_ref[slab % 2] = jnp.broadcast_to(top, (SLAB * rows, HD))

        def weigh(slab):
            top = top_ref[slab % 2]
            weights = [
                jnp.exp2((s_ref[slab % 2, :, i * HD : (i + 1) * HD] - top) * scale).astype(
                    jnp.bfloat16
                )
                for i in range(len(keys) * step // HD)
            ]
            acc = jnp.dot(
                jnp.concatenate(weights, axis=1), values, preferred_element_type=jnp.float32
            )
            out = (acc[:, :HD] / acc[:, HD:]).astype(o_ref.dtype)
            for j in range(SLAB):
                g = slab * SLAB + j
                o_ref[:, g * HD : (g + 1) * HD] = out[j * rows : (j + 1) * rows]

        score(0)
        for slab in range(GQ // SLAB):
            if slab + 1 < GQ // SLAB:
                score(slab + 1)
            weigh(slab)

    for near in range(pairs):
        pl.when(reach == near)(functools.partial(body, near))


def attend(meta, seg_q, seg_k, prefix_bias, queries, pieces, prefix, out):
    rows = queries.shape[0]
    prefix_keys = prefix.shape[0]
    pairs = len(pieces) // 2
    heads = pieces[0].shape[1] // (2 * HD)
    wide = (rows, GQ * HD)
    in_specs = [
        pl.BlockSpec((rows, 1), lambda i, m: (0, 0)),
        pl.BlockSpec(seg_k.shape, lambda i, m: (0, 0, 0)),
        pl.BlockSpec((1, prefix_keys), lambda i, m: (0, 0)),
        pl.BlockSpec(wide, lambda i, m: (0, m[2] + i)),
        pl.BlockSpec((prefix_keys, HD), lambda i, m: (0, i)),
        pl.BlockSpec((prefix_keys, HD), lambda i, m: (0, heads + i)),
        *[pl.BlockSpec((rows, HD), lambda i, m: (0, i))] * len(pieces),
        *[pl.BlockSpec((rows, HD), lambda i, m: (0, heads + i))] * len(pieces),
    ]
    args = [meta, seg_q, seg_k, prefix_bias, queries, prefix, prefix, *pieces, *pieces]
    aliases = {}
    if out is not None:
        in_specs.append(pl.BlockSpec(memory_space=pl.ANY))
        args.append(out)
        aliases = {len(args) - 1: 0}
    all_keys = 2 * rows * pairs + prefix_keys
    return pl.pallas_call(
        functools.partial(attend_kernel, pairs),
        grid_spec=pltpu.PrefetchScalarGridSpec(
            num_scalar_prefetch=1,
            grid=(heads,),
            in_specs=in_specs,
            out_specs=pl.BlockSpec(wide, lambda i, m: (0, m[2] + i)),
            scratch_shapes=[
                pltpu.VMEM((2, SLAB * rows, all_keys), jnp.float32),
                pltpu.VMEM((2, SLAB * rows, HD), jnp.float32),
                pltpu.VMEM((pairs, rows, 2 * rows), jnp.float32),
            ],
        ),
        out_shape=jax.ShapeDtypeStruct(queries.shape, queries.dtype),
        input_output_aliases=aliases,
        compiler_params=pltpu.CompilerParams(vmem_limit_bytes=40 * 1024 * 1024),
    )(*args)


def on_device(queries, resp_kv, resp_segments, prefix_kv, tile_plan, prompt_lengths):
    rows = queries.shape[1]
    half = KVH * HD // 2
    tiles, tile = prefix_kv.shape[:2]
    groups, count = lax.axis_size("prompt"), lax.axis_size("resp")
    per = tiles // groups
    group = lax.axis_index("prompt")
    block = lax.axis_index("resp")
    side = block % 2
    steps = min(count // 2 - 1, (REACH + 1) // 2)

    def part(owner):
        kv = resp_kv[0].reshape(rows, 2, 2, half)
        return lax.dynamic_index_in_dim(kv, owner, 2, keepdims=False).reshape(rows, 2 * half)

    def swap(value, first):
        return lax.ppermute(value, "resp", [(r, r ^ 1) for r in range(2 * first, count)])

    def climb(value, step):
        pairs = [(r, r + 2) for r in range(2 * step - 2, count - 2)]
        return lax.ppermute(value, "resp", pairs)

    mine, theirs = part(side), part(1 - side)
    straight = [mine, swap(theirs, 0)]
    upper = lax.ppermute(mine, "resp", [(r, r + 1) for r in range(0, count, 2)])
    crossed = [theirs, upper]

    owner, place = tile_plan[:, 0], tile_plan[:, 1]
    index = jnp.arange(tiles, dtype=jnp.int32)
    ahead = (owner[None, :] < owner[:, None]) | (
        (owner[None, :] == owner[:, None]) & (index[None, :] < index[:, None])
    )
    pick = jnp.sum(ahead, axis=1, dtype=jnp.int32)[None, :] == index[:, None]
    own_place = jnp.sum(jnp.where(pick, place[None, :], 0), axis=1, dtype=jnp.int32)
    own_tiles = jnp.sum(
        jnp.where(pick[:, :, None, None], prefix_kv[None], 0).astype(jnp.float32), axis=1
    )
    own_tiles = own_tiles.reshape(groups, per, tile, 2, 2, half).transpose(0, 4, 1, 2, 3, 5)
    own_tiles = own_tiles.reshape(groups, 2, per, tile, 2 * half)
    row = jnp.arange(tile, dtype=jnp.int32)[:, None]
    extra = jnp.where(
        row == 0, resp_segments[0], own_place.reshape(groups, 1, per, 1, 1)
    ).astype(jnp.float32)
    extra = jnp.broadcast_to(extra, (groups, 2, per, tile, rows))
    out_tiles = jnp.concatenate([own_tiles, extra], axis=-1).astype(prefix_kv.dtype)
    out_tiles = jnp.broadcast_to(
        out_tiles[:, None], (groups, count // 2, *out_tiles.shape[1:])
    ).reshape(groups * count, per * tile, 2 * half + rows)
    came = lax.all_to_all(
        out_tiles, ("prompt", "resp"), split_axis=0, concat_axis=0, tiled=True
    )
    prefix = came.reshape(-1, 2 * half + rows)
    prefix_crossed = swap(prefix, 0)

    for step in range(1, steps + 1):
        for k in range(2):
            straight.append(climb(straight[-2], step))
        crossed += [swap(straight[-1], step), swap(straight[-2], step)]

    ints = came.reshape(groups, count, per, tile, -1)[..., 2 * half :].astype(jnp.int32)
    seg_k = lax.dynamic_index_in_dim(ints[:, :, 0, 0], group, 0, keepdims=False)
    places = ints[:, :, :, 1, :1].reshape(-1, 1) * tile + row.reshape(1, -1)
    prefix_bias = jnp.where(places < prompt_lengths[0], 0.0, FILL).reshape(1, -1)
    seg_q = resp_segments[0][:, None]
    before = jnp.sum(seg_k < resp_segments[0, 0], dtype=jnp.int32)
    reach = block // 2 - before // (2 * rows)
    seg_k = seg_k[:, None, :]

    out = None
    for first, pieces, tiles_of in (
        (side, straight, prefix),
        (1 - side, crossed, prefix_crossed),
    ):
        meta = jnp.stack([block, reach, first * (KVH // 2)])
        out = attend(meta, seg_q, seg_k, prefix_bias, queries[0], pieces, tiles_of, out)
    return out[None]


def solution(mesh):
    return jax.shard_map(
        on_device,
        mesh=mesh,
        in_specs=(
            P("prompt", "resp", None),
            P("prompt", "resp", None),
            P("prompt", "resp"),
            P(("prompt", "resp"), None, None),
            P(("prompt", "resp"), None),
            P("prompt"),
        ),
        out_specs=P("prompt", "resp", None),
        check_vma=False,
    )
```

```python
import functools
import math

import jax
import jax.numpy as jnp
from jax import lax
from jax.experimental import pallas as pl
from jax.experimental.pallas import tpu as pltpu
from jax.sharding import PartitionSpec as P

H = 64
KVH = 8
HD = 128
GQ = H // KVH
REACH = 7
SLAB = 2
FILL = -1e30


def attend_kernel(pairs, meta_ref, seg_q_ref, seg_k_ref, prefix_bias_ref, q_ref, pk_ref, pv_ref, *rest):
    k_refs, v_refs = rest[: 2 * pairs], rest[2 * pairs : 4 * pairs]
    o_ref, s_ref, top_ref, bias_ref = rest[-4:]
    rows = q_ref.shape[0]
    step = 2 * rows
    prefix_steps = pk_ref.shape[0] // step
    block, reach = meta_ref[0], meta_ref[1]
    scale = math.log2(math.e) / math.sqrt(HD)
    nt = (((1,), (1,)), ((), ()))

    @pl.when(pl.program_id(0) == 0)
    def _():
        row_pos = block * rows + lax.broadcasted_iota(jnp.int32, (rows, rows), 0)
        lane = lax.broadcasted_iota(jnp.int32, (rows, rows), 1)
        for k in range(pairs):
            for part, first in enumerate((block, block + 1 - 2 * lax.rem(block, 2))):
                key_block = jnp.maximum(first - 2 * k, 0)
                seen = (seg_k_ref[key_block] == seg_q_ref[...]) & (
                    key_block * rows + lane <= row_pos
                )
                bias_ref[k, :, part * rows : (part + 1) * rows] = jnp.where(seen, 0.0, FILL)

    def body(near):
        keys = [pk_ref[i * step : (i + 1) * step, :] for i in range(prefix_steps)]
        values = [pv_ref[i * step : (i + 1) * step, :] for i in range(prefix_steps)]
        for k in range(near + 1):
            keys.append(jnp.concatenate([k_refs[2 * k][...], k_refs[2 * k + 1][...]]))
            values.append(jnp.concatenate([v_refs[2 * k][...], v_refs[2 * k + 1][...]]))
        values = jnp.concatenate(values)
        values = jnp.concatenate([values, jnp.ones_like(values)], axis=1)

        def score(slab):
            heads = range(slab * SLAB, (slab + 1) * SLAB)
            q = jnp.concatenate([q_ref[:, g * HD : (g + 1) * HD] for g in heads])
            top = None
            for i, key in enumerate(keys):
                s = lax.dot_general(q, key, nt, preferred_element_type=jnp.float32)
                if i < prefix_steps:
                    bias = prefix_bias_ref[:, i * step : (i + 1) * step]
                else:
                    bias = bias_ref[i - prefix_steps]
                s = (s.reshape(SLAB, rows, step) + bias[None]).reshape(SLAB * rows, step)
                s_ref[slab % 2, :, i * step : (i + 1) * step] = s
                high = jnp.maximum(s[:, :rows], s[:, rows:])
                top = high if top is None else jnp.maximum(top, high)
            top = jnp.max(top, axis=1, keepdims=True)
            top_ref[slab % 2] = jnp.broadcast_to(top, (SLAB * rows, HD))

        def weigh(slab):
            top = top_ref[slab % 2]
            weights = [
                jnp.exp2((s_ref[slab % 2, :, i * HD : (i + 1) * HD] - top) * scale).astype(
                    jnp.bfloat16
                )
                for i in range(len(keys) * step // HD)
            ]
            acc = jnp.dot(
                jnp.concatenate(weights, axis=1), values, preferred_element_type=jnp.float32
            )
            out = (acc[:, :HD] / acc[:, HD:]).astype(o_ref.dtype)
            for j in range(SLAB):
                g = slab * SLAB + j
                o_ref[:, g * HD : (g + 1) * HD] = out[j * rows : (j + 1) * rows]

        score(0)
        for slab in range(GQ // SLAB):
            if slab + 1 < GQ // SLAB:
                score(slab + 1)
            weigh(slab)

    for near in range(pairs):
        pl.when(reach == near)(functools.partial(body, near))


def attend(meta, seg_q, seg_k, prefix_bias, queries, pieces, prefix, out):
    rows = queries.shape[0]
    prefix_keys = prefix.shape[0]
    pairs = len(pieces) // 2
    heads = pieces[0].shape[1] // (2 * HD)
    wide = (rows, GQ * HD)
    in_specs = [
        pl.BlockSpec((rows, 1), lambda i, m: (0, 0)),
        pl.BlockSpec(seg_k.shape, lambda i, m: (0, 0, 0)),
        pl.BlockSpec((1, prefix_keys), lambda i, m: (0, 0)),
        pl.BlockSpec(wide, lambda i, m: (0, m[2] + i)),
        pl.BlockSpec((prefix_keys, HD), lambda i, m: (0, m[2] + i)),
        pl.BlockSpec((prefix_keys, HD), lambda i, m: (0, KVH + m[2] + i)),
        *[pl.BlockSpec((rows, HD), lambda i, m: (0, i))] * len(pieces),
        *[pl.BlockSpec((rows, HD), lambda i, m: (0, heads + i))] * len(pieces),
    ]
    args = [meta, seg_q, seg_k, prefix_bias, queries, prefix, prefix, *pieces, *pieces]
    aliases = {}
    if out is not None:
        in_specs.append(pl.BlockSpec(memory_space=pl.ANY))
        args.append(out)
        aliases = {len(args) - 1: 0}
    all_keys = 2 * rows * pairs + prefix_keys
    return pl.pallas_call(
        functools.partial(attend_kernel, pairs),
        grid_spec=pltpu.PrefetchScalarGridSpec(
            num_scalar_prefetch=1,
            grid=(heads,),
            in_specs=in_specs,
            out_specs=pl.BlockSpec(wide, lambda i, m: (0, m[2] + i)),
            scratch_shapes=[
                pltpu.VMEM((2, SLAB * rows, all_keys), jnp.float32),
                pltpu.VMEM((2, SLAB * rows, HD), jnp.float32),
                pltpu.VMEM((pairs, rows, 2 * rows), jnp.float32),
            ],
        ),
        out_shape=jax.ShapeDtypeStruct(queries.shape, queries.dtype),
        input_output_aliases=aliases,
        compiler_params=pltpu.CompilerParams(vmem_limit_bytes=40 * 1024 * 1024),
    )(*args)


def on_device(queries, resp_kv, resp_segments, prefix_kv, tile_plan, prompt_lengths):
    rows = queries.shape[1]
    half = KVH * HD // 2
    tiles, tile = prefix_kv.shape[:2]
    groups, count = lax.axis_size("prompt"), lax.axis_size("resp")
    per = tiles // groups
    group = lax.axis_index("prompt")
    block = lax.axis_index("resp")
    side = block % 2
    steps = min(count // 2 - 1, (REACH + 1) // 2)

    def part(owner):
        k = lax.dynamic_slice_in_dim(resp_kv[0], owner * half, half, 1)
        v = lax.dynamic_slice_in_dim(resp_kv[0], (2 + owner) * half, half, 1)
        return jnp.concatenate([k, v], axis=1)

    def swap(value, first):
        return lax.ppermute(value, "resp", [(r, r ^ 1) for r in range(2 * first, count)])

    def climb(value, step):
        pairs = [(r, r + 2) for r in range(2 * step - 2, count - 2)]
        return lax.ppermute(value, "resp", pairs)

    mine, theirs = part(side), part(1 - side)
    straight = [mine, swap(theirs, 0)]
    crossed = [theirs, None]

    owner, place = tile_plan[:, 0], tile_plan[:, 1]
    index = jnp.arange(tiles, dtype=jnp.int32)
    ahead = (owner[None, :] < owner[:, None]) | (
        (owner[None, :] == owner[:, None]) & (index[None, :] < index[:, None])
    )
    pick = jnp.sum(ahead, axis=1, dtype=jnp.int32)[None, :] == index[:, None]
    own_place = jnp.sum(jnp.where(pick, place[None, :], 0), axis=1, dtype=jnp.int32)
    own_tiles = jnp.sum(
        jnp.where(pick[:, :, None, None], prefix_kv[None], 0).astype(jnp.float32), axis=1
    )
    own_tiles = own_tiles.reshape(groups, per, tile, 4 * half)
    row = jnp.arange(tile, dtype=jnp.int32)[:, None]
    extra = jnp.where(row == 0, resp_segments[0], own_place.reshape(groups, per, 1, 1))
    extra = jnp.broadcast_to(extra.astype(jnp.float32), (groups, per, tile, rows))
    out_tiles = jnp.concatenate([own_tiles, extra], axis=-1).astype(prefix_kv.dtype)
    out_tiles = jnp.broadcast_to(
        out_tiles[:, None], (groups, count, *out_tiles.shape[1:])
    ).reshape(groups * count, per * tile, 4 * half + rows)
    out_tiles, straight[1] = lax.optimization_barrier((out_tiles, straight[1]))
    came = lax.all_to_all(
        out_tiles, ("prompt", "resp"), split_axis=0, concat_axis=0, tiled=True
    )
    for step in range(1, steps + 1):
        for k in range(2):
            source = straight[-2]
            if step > 2:
                late = 2 * (step - 2) + 1 - k
                source, crossed[late] = lax.optimization_barrier((source, crossed[late]))
            straight.append(climb(source, step))
        crossed += [swap(straight[-1], step), swap(straight[-2], step)]

    mine, straight[3] = lax.optimization_barrier((mine, straight[3]))
    crossed[1] = lax.ppermute(mine, "resp", [(r, r + 1) for r in range(0, count, 2)])
    came, straight[-3] = lax.optimization_barrier((came, straight[-3]))
    prefix = came.reshape(-1, 4 * half + rows)
    ints = came.reshape(groups, count, per, tile, -1)[..., 4 * half :].astype(jnp.int32)
    seg_k = lax.dynamic_index_in_dim(ints[:, :, 0, 0], group, 0, keepdims=False)
    places = ints[:, :, :, 1, :1].reshape(-1, 1) * tile + row.reshape(1, -1)
    prefix_bias = jnp.where(places < prompt_lengths[0], 0.0, FILL).reshape(1, -1)
    seg_q = resp_segments[0][:, None]
    before = jnp.sum(seg_k < resp_segments[0, 0], dtype=jnp.int32)
    reach = block // 2 - before // (2 * rows)
    seg_k = seg_k[:, None, :]

    out = None
    for first, pieces in ((side, straight), (1 - side, crossed)):
        meta = jnp.stack([block, reach, first * (KVH // 2)])
        out = attend(meta, seg_q, seg_k, prefix_bias, queries[0], pieces, prefix, out)
    return out[None]


def solution(mesh):
    return jax.shard_map(
        on_device,
        mesh=mesh,
        in_specs=(
            P("prompt", "resp", None),
            P("prompt", "resp", None),
            P("prompt", "resp"),
            P(("prompt", "resp"), None, None),
            P(("prompt", "resp"), None),
            P("prompt"),
        ),
        out_specs=P("prompt", "resp", None),
        check_vma=False,
    )
```

```python
import functools
import math

import jax
import jax.numpy as jnp
from jax import lax
from jax.experimental import pallas as pl
from jax.experimental.pallas import tpu as pltpu
from jax.sharding import PartitionSpec as P

H = 64
KVH = 8
HD = 128
GQ = H // KVH
REACH = 7
SLAB = 2
FILL = -1e30


def halves_kernel(meta_ref, a_ref, b_ref, mine_ref, theirs_ref):
    mine_ref[...] = a_ref[...]
    theirs_ref[...] = b_ref[...]


def halves(kv, side):
    rows, half = kv.shape[0], kv.shape[1] // 4
    shape = (rows, half)
    return pl.pallas_call(
        halves_kernel,
        grid_spec=pltpu.PrefetchScalarGridSpec(
            num_scalar_prefetch=1,
            grid=(2,),
            in_specs=[
                pl.BlockSpec(shape, lambda i, m: (0, 2 * i + m[0])),
                pl.BlockSpec(shape, lambda i, m: (0, 2 * i + 1 - m[0])),
            ],
            out_specs=[pl.BlockSpec(shape, lambda i, m: (0, i))] * 2,
        ),
        out_shape=[jax.ShapeDtypeStruct((rows, 2 * half), kv.dtype)] * 2,
    )(side.reshape(1), kv, kv)


def attend_kernel(pairs, tile, count, meta_ref, seg_ref, q_ref, prefix_ref, *rest):
    pieces = rest[: 2 * pairs]
    o_ref, k_ref, v_ref, ints_ref, seg_k_ref, bias_ref, s_ref, top_ref, reach_ref, sems, sem = (
        rest[-11:]
    )
    rows = q_ref.shape[0]
    heads = k_ref.shape[0]
    step = 2 * rows
    prefix_keys = prefix_ref.shape[0]
    group, block, head0, limit = meta_ref[0], meta_ref[1], meta_ref[2], meta_ref[3]
    head = pl.program_id(0)
    scale = math.log2(math.e) / math.sqrt(HD)
    nt = (((1,), (1,)), ((), ()))

    def column(index):
        return pl.ds(pl.multiple_of(index * HD, HD), HD)

    def copies(h):
        sources = [(prefix_ref, head0 + h, KVH + head0 + h, 0, prefix_keys)]
        for j, piece in enumerate(pieces):
            sources.append((piece, h, heads + h, prefix_keys + j * rows, rows))
        for j, (ref, k_at, v_at, start, size) in enumerate(sources):
            at = pl.ds(start, size)
            yield pltpu.make_async_copy(
                ref.at[:, column(k_at)], k_ref.at[h, at], sems.at[h, 2 * j]
            )
            yield pltpu.make_async_copy(
                ref.at[:, column(v_at)], v_ref.at[h, at, pl.ds(0, HD)], sems.at[h, 2 * j + 1]
            )

    @pl.when(head == 0)
    def _():
        ints_copy = pltpu.make_async_copy(
            prefix_ref.at[:, pl.ds(2 * KVH * HD, rows)], ints_ref, sem
        )
        ints_copy.start()
        for h in range(heads):
            for copy in copies(h):
                copy.start()
        v_ref[:, :, HD:] = jnp.ones((heads, v_ref.shape[1], HD), v_ref.dtype)
        ints_copy.wait()
        ints = ints_ref[...].astype(jnp.float32)
        seg_k_ref[...] = ints
        part = lax.rem(lax.broadcasted_iota(jnp.int32, ints.shape, 0), tile)
        place = jnp.where(part == 0, pltpu.roll(ints, prefix_keys - 1, 0), ints)
        live = place.astype(jnp.int32) * tile + part < limit
        bias_ref[:, :prefix_keys] = jnp.where(live, 0.0, FILL).T

        own = seg_ref[...].astype(jnp.float32)
        first_key = group * count * tile
        segs = seg_k_ref[pl.ds(pl.multiple_of(first_key, tile), count * tile), :]
        heads_of = lax.rem(lax.broadcasted_iota(jnp.int32, segs.shape, 0), tile) == 0
        earlier = jnp.sum(jnp.where(heads_of & (segs < own[:, :1]), 1.0, 0.0))
        reach_ref[0] = lax.div(block, 2) - lax.div(earlier.astype(jnp.int32), step)

        seg_q = jnp.broadcast_to(own, (rows, rows)).T
        row_pos = block * rows + lax.broadcasted_iota(jnp.int32, (rows, rows), 0)
        lane = lax.broadcasted_iota(jnp.int32, (rows, rows), 1)
        for k in range(pairs):
            for j, first in enumerate((block, block + 1 - 2 * lax.rem(block, 2))):
                key_block = jnp.maximum(first - 2 * k, 0)
                at = pl.multiple_of(first_key + key_block * tile, tile)
                seg_k = seg_k_ref[pl.ds(at, tile), :][:1]
                seen = (seg_k == seg_q) & (key_block * rows + lane <= row_pos)
                at = prefix_keys + (2 * k + j) * rows
                bias_ref[:, at : at + rows] = jnp.where(seen, 0.0, FILL)

    for copy in copies(head):
        copy.wait()

    def body(near):
        steps = prefix_keys // step + near + 1

        def score(slab):
            of = range(slab * SLAB, (slab + 1) * SLAB)
            q = jnp.concatenate([q_ref[:, g * HD : (g + 1) * HD] for g in of])
            top = None
            for i in range(steps):
                at = slice(i * step, (i + 1) * step)
                s = lax.dot_general(q, k_ref[head, at, :], nt, preferred_element_type=jnp.float32)
                s = (s.reshape(SLAB, rows, step) + bias_ref[:, at][None]).reshape(-1, step)
                s_ref[slab % 2, :, at] = s
                high = jnp.maximum(s[:, :rows], s[:, rows:])
                top = high if top is None else jnp.maximum(top, high)
            top = jnp.max(top, axis=1, keepdims=True)
            top_ref[slab % 2] = jnp.broadcast_to(top, (SLAB * rows, HD))

        def weigh(slab):
            top = top_ref[slab % 2]
            weights = [
                jnp.exp2((s_ref[slab % 2, :, i * HD : (i + 1) * HD] - top) * scale).astype(
                    jnp.bfloat16
                )
                for i in range(steps * step // HD)
            ]
            acc = jnp.dot(
                jnp.concatenate(weights, axis=1),
                v_ref[head, : steps * step, :],
                preferred_element_type=jnp.float32,
            )
            out = (acc[:, :HD] / acc[:, HD:]).astype(o_ref.dtype)
            for j in range(SLAB):
                g = slab * SLAB + j
                o_ref[:, g * HD : (g + 1) * HD] = out[j * rows : (j + 1) * rows]

        score(0)
        for slab in range(GQ // SLAB):
            if slab + 1 < GQ // SLAB:
                score(slab + 1)
            weigh(slab)

    for near in range(pairs):
        pl.when(reach_ref[0] == near)(functools.partial(body, near))


def attend(meta, segments, queries, pieces, prefix, tile, count, out):
    rows = queries.shape[0]
    prefix_keys = prefix.shape[0]
    pairs = len(pieces) // 2
    heads = pieces[0].shape[1] // (2 * HD)
    keys = rows * len(pieces) + prefix_keys
    wide = (rows, GQ * HD)
    far = pl.BlockSpec(memory_space=pl.ANY)
    in_specs = [
        pl.BlockSpec((1, rows), lambda i, m: (0, 0)),
        pl.BlockSpec(wide, lambda i, m: (0, m[2] + i)),
        far,
        *[far] * len(pieces),
    ]
    args = [meta, segments, queries, prefix, *pieces]
    aliases = {}
    if out is not None:
        in_specs.append(far)
        args.append(out)
        aliases = {len(args) - 1: 0}
    return pl.pallas_call(
        functools.partial(attend_kernel, pairs, tile, count),
        grid_spec=pltpu.PrefetchScalarGridSpec(
            num_scalar_prefetch=1,
            grid=(heads,),
            in_specs=in_specs,
            out_specs=pl.BlockSpec(wide, lambda i, m: (0, m[2] + i)),
            scratch_shapes=[
                pltpu.VMEM((heads, keys, HD), queries.dtype),
                pltpu.VMEM((heads, keys, 2 * HD), queries.dtype),
                pltpu.VMEM((prefix_keys, rows), queries.dtype),
                pltpu.VMEM((prefix_keys, rows), jnp.float32),
                pltpu.VMEM((rows, keys), jnp.float32),
                pltpu.VMEM((2, SLAB * rows, keys), jnp.float32),
                pltpu.VMEM((2, SLAB * rows, HD), jnp.float32),
                pltpu.SMEM((1,), jnp.int32),
                pltpu.SemaphoreType.DMA((heads, 2 * (len(pieces) + 1))),
                pltpu.SemaphoreType.DMA(()),
            ],
        ),
        out_shape=jax.ShapeDtypeStruct(queries.shape, queries.dtype),
        input_output_aliases=aliases,
        compiler_params=pltpu.CompilerParams(vmem_limit_bytes=40 * 1024 * 1024),
    )(*args)


def on_device(queries, resp_kv, resp_segments, prefix_kv, tile_plan, prompt_lengths):
    rows = queries.shape[1]
    tiles, tile, columns = prefix_kv.shape
    groups, count = lax.axis_size("prompt"), lax.axis_size("resp")
    group = lax.axis_index("prompt")
    block = lax.axis_index("resp")
    side = block % 2
    steps = min(count // 2 - 1, (REACH + 1) // 2)
    assert tiles == groups

    def swap(value, first):
        return lax.ppermute(value, "resp", [(r, r ^ 1) for r in range(2 * first, count)])

    def climb(value, step):
        pairs = [(r, r + 2) for r in range(2 * step - 2, count - 2)]
        return lax.ppermute(value, "resp", pairs)

    mine, theirs = halves(resp_kv[0], side)
    straight = [mine, swap(theirs, 0), climb(mine, 1)]
    crossed = [theirs, lax.ppermute(mine, "resp", [(r, r + 1) for r in range(0, count, 2)])]

    pick = tile_plan[None, :, 0] == jnp.arange(groups, dtype=jnp.int32)[:, None]
    place = jnp.sum(jnp.where(pick, tile_plan[None, :, 1], 0), axis=1, dtype=jnp.int32)
    own_tiles = jnp.sum(
        jnp.where(pick[:, :, None, None], prefix_kv[None], 0).astype(jnp.float32), axis=1
    )
    row = jnp.arange(tile, dtype=jnp.int32)[:, None]
    extra = jnp.where(row == 0, resp_segments[0], place.reshape(groups, 1, 1))
    out_tiles = jnp.concatenate([own_tiles, extra.astype(jnp.float32)], axis=-1)
    out_tiles = jnp.broadcast_to(
        out_tiles.astype(prefix_kv.dtype)[:, None], (groups, count, tile, columns + rows)
    ).reshape(groups * count, tile, columns + rows)
    out_tiles, straight[2] = lax.optimization_barrier((out_tiles, straight[2]))
    came = lax.all_to_all(
        out_tiles, ("prompt", "resp"), split_axis=0, concat_axis=0, tiled=True
    )
    prefix = came.reshape(-1, columns + rows)

    for step in range(1, steps + 1):
        for k in range(2):
            if step + k == 1:
                continue
            source = straight[-2]
            late = 1 if step == 2 else 2 * (step - 2) + 1 - k
            if step > 2 or step + k == 3:
                source, crossed[late] = lax.optimization_barrier((source, crossed[late]))
            straight.append(climb(source, step))
        crossed += [swap(straight[-1], step), swap(straight[-2], step)]

    out = None
    for first, pieces in ((side, straight), (1 - side, crossed)):
        meta = jnp.stack([group, block, first * (KVH // 2), prompt_lengths[0]])
        out = attend(meta, resp_segments, queries[0], pieces, prefix, tile, count, out)
    return out[None]


def solution(mesh):
    return jax.shard_map(
        on_device,
        mesh=mesh,
        in_specs=(
            P("prompt", "resp", None),
            P("prompt", "resp", None),
            P("prompt", "resp"),
            P(("prompt", "resp"), None, None),
            P(("prompt", "resp"), None),
            P("prompt"),
        ),
        out_specs=P("prompt", "resp", None),
        check_vma=False,
    )
```

```python
import functools
import math

import jax
import jax.numpy as jnp
from jax import lax
from jax.experimental import pallas as pl
from jax.experimental.pallas import tpu as pltpu
from jax.sharding import PartitionSpec as P

H = 64
KVH = 8
HD = 128
GQ = H // KVH
REACH = 7
SLAB = 2
FILL = -1e30


def halves_kernel(meta_ref, a_ref, b_ref, mine_ref, theirs_ref):
    mine_ref[...] = a_ref[...]
    theirs_ref[...] = b_ref[...]


def halves(kv, side):
    rows, half = kv.shape[0], kv.shape[1] // 4
    shape = (rows, half)
    return pl.pallas_call(
        halves_kernel,
        grid_spec=pltpu.PrefetchScalarGridSpec(
            num_scalar_prefetch=1,
            grid=(2,),
            in_specs=[
                pl.BlockSpec(shape, lambda i, m: (0, 2 * i + m[0])),
                pl.BlockSpec(shape, lambda i, m: (0, 2 * i + 1 - m[0])),
            ],
            out_specs=[pl.BlockSpec(shape, lambda i, m: (0, i))] * 2,
        ),
        out_shape=[jax.ShapeDtypeStruct((rows, 2 * half), kv.dtype)] * 2,
    )(side.reshape(1), kv, kv)


def attend_kernel(pairs, tile, count, meta_ref, seg_ref, q_ref, prefix_ref, *rest):
    pieces = rest[: 2 * pairs]
    o_ref, k_ref, v_ref, ints_ref, seg_k_ref, bias_ref, s_ref, top_ref, reach_ref, sems, sem = (
        rest[-11:]
    )
    rows = q_ref.shape[0]
    heads = k_ref.shape[0]
    step = 2 * rows
    prefix_keys = prefix_ref.shape[0]
    group, block, head0, limit = meta_ref[0], meta_ref[1], meta_ref[2], meta_ref[3]
    head = pl.program_id(0)
    scale = math.log2(math.e) / math.sqrt(HD)
    nt = (((1,), (1,)), ((), ()))

    def column(index):
        return pl.ds(pl.multiple_of(index * HD, HD), HD)

    def copies(h):
        sources = [(prefix_ref, head0 + h, KVH + head0 + h, 0, prefix_keys)]
        for j, piece in enumerate(pieces):
            sources.append((piece, h, heads + h, prefix_keys + j * rows, rows))
        for j, (ref, k_at, v_at, start, size) in enumerate(sources):
            at = pl.ds(start, size)
            yield pltpu.make_async_copy(
                ref.at[:, column(k_at)], k_ref.at[h, at], sems.at[h, 2 * j]
            )
            yield pltpu.make_async_copy(
                ref.at[:, column(v_at)], v_ref.at[h, at, pl.ds(0, HD)], sems.at[h, 2 * j + 1]
            )

    @pl.when(head == 0)
    def _():
        ints_copy = pltpu.make_async_copy(
            prefix_ref.at[:, pl.ds(2 * KVH * HD, rows)], ints_ref, sem
        )
        ints_copy.start()
        for h in range(heads):
            for copy in copies(h):
                copy.start()
        v_ref[:, :, HD:] = jnp.ones((heads, v_ref.shape[1], HD), v_ref.dtype)
        ints_copy.wait()
        ints = ints_ref[...].astype(jnp.float32)
        seg_k_ref[...] = ints
        part = lax.rem(lax.broadcasted_iota(jnp.int32, ints.shape, 0), tile)
        place = jnp.where(part == 0, pltpu.roll(ints, prefix_keys - 1, 0), ints)
        live = place.astype(jnp.int32) * tile + part < limit
        bias_ref[:, :prefix_keys] = jnp.where(live, 0.0, FILL).T

        own = seg_ref[...].astype(jnp.float32)
        first_key = group * count * tile
        segs = seg_k_ref[pl.ds(pl.multiple_of(first_key, tile), count * tile), :]
        heads_of = lax.rem(lax.broadcasted_iota(jnp.int32, segs.shape, 0), tile) == 0
        earlier = jnp.sum(jnp.where(heads_of & (segs < own[:, :1]), 1.0, 0.0))
        reach_ref[0] = lax.div(block, 2) - lax.div(earlier.astype(jnp.int32), step)

        seg_q = jnp.broadcast_to(own, (rows, rows)).T
        row_pos = block * rows + lax.broadcasted_iota(jnp.int32, (rows, rows), 0)
        lane = lax.broadcasted_iota(jnp.int32, (rows, rows), 1)
        for k in range(pairs):
            for j, first in enumerate((block, block + 1 - 2 * lax.rem(block, 2))):
                key_block = jnp.maximum(first - 2 * k, 0)
                at = pl.multiple_of(first_key + key_block * tile, tile)
                seg_k = seg_k_ref[pl.ds(at, tile), :][:1]
                seen = (seg_k == seg_q) & (key_block * rows + lane <= row_pos)
                at = prefix_keys + (2 * k + j) * rows
                bias_ref[:, at : at + rows] = jnp.where(seen, 0.0, FILL)

    for copy in copies(head):
        copy.wait()

    def body(near):
        steps = prefix_keys // step + near + 1

        def score(slab):
            of = range(slab * SLAB, (slab + 1) * SLAB)
            q = jnp.concatenate([q_ref[:, g * HD : (g + 1) * HD] for g in of])
            top = None
            for i in range(steps):
                at = slice(i * step, (i + 1) * step)
                s = lax.dot_general(q, k_ref[head, at, :], nt, preferred_element_type=jnp.float32)
                s = (s.reshape(SLAB, rows, step) + bias_ref[:, at][None]).reshape(-1, step)
                s_ref[slab % 2, :, at] = s
                high = jnp.maximum(s[:, :rows], s[:, rows:])
                top = high if top is None else jnp.maximum(top, high)
            top = jnp.max(top, axis=1, keepdims=True)
            top_ref[slab % 2] = jnp.broadcast_to(top, (SLAB * rows, HD))

        def weigh(slab):
            top = top_ref[slab % 2]
            weights = [
                jnp.exp2((s_ref[slab % 2, :, i * HD : (i + 1) * HD] - top) * scale).astype(
                    jnp.bfloat16
                )
                for i in range(steps * step // HD)
            ]
            acc = jnp.dot(
                jnp.concatenate(weights, axis=1),
                v_ref[head, : steps * step, :],
                preferred_element_type=jnp.float32,
            )
            out = (acc[:, :HD] / acc[:, HD:]).astype(o_ref.dtype)
            for j in range(SLAB):
                g = slab * SLAB + j
                o_ref[:, g * HD : (g + 1) * HD] = out[j * rows : (j + 1) * rows]

        score(0)
        for slab in range(GQ // SLAB):
            if slab + 1 < GQ // SLAB:
                score(slab + 1)
            weigh(slab)

    for near in range(pairs):
        pl.when(reach_ref[0] == near)(functools.partial(body, near))


def attend(meta, segments, queries, pieces, prefix, tile, count, out):
    rows = queries.shape[0]
    prefix_keys = prefix.shape[0]
    pairs = len(pieces) // 2
    heads = pieces[0].shape[1] // (2 * HD)
    keys = rows * len(pieces) + prefix_keys
    wide = (rows, GQ * HD)
    far = pl.BlockSpec(memory_space=pl.ANY)
    in_specs = [
        pl.BlockSpec((1, rows), lambda i, m: (0, 0)),
        pl.BlockSpec(wide, lambda i, m: (0, m[2] + i)),
        far,
        *[far] * len(pieces),
    ]
    args = [meta, segments, queries, prefix, *pieces]
    aliases = {}
    if out is not None:
        in_specs.append(far)
        args.append(out)
        aliases = {len(args) - 1: 0}
    return pl.pallas_call(
        functools.partial(attend_kernel, pairs, tile, count),
        grid_spec=pltpu.PrefetchScalarGridSpec(
            num_scalar_prefetch=1,
            grid=(heads,),
            in_specs=in_specs,
            out_specs=pl.BlockSpec(wide, lambda i, m: (0, m[2] + i)),
            scratch_shapes=[
                pltpu.VMEM((heads, keys, HD), queries.dtype),
                pltpu.VMEM((heads, keys, 2 * HD), queries.dtype),
                pltpu.VMEM((prefix_keys, rows), queries.dtype),
                pltpu.VMEM((prefix_keys, rows), jnp.float32),
                pltpu.VMEM((rows, keys), jnp.float32),
                pltpu.VMEM((2, SLAB * rows, keys), jnp.float32),
                pltpu.VMEM((2, SLAB * rows, HD), jnp.float32),
                pltpu.SMEM((1,), jnp.int32),
                pltpu.SemaphoreType.DMA((heads, 2 * (len(pieces) + 1))),
                pltpu.SemaphoreType.DMA(()),
            ],
        ),
        out_shape=jax.ShapeDtypeStruct(queries.shape, queries.dtype),
        input_output_aliases=aliases,
        compiler_params=pltpu.CompilerParams(vmem_limit_bytes=20 * 1024 * 1024),
    )(*args)


def on_device(queries, resp_kv, resp_segments, prefix_kv, tile_plan, prompt_lengths):
    rows = queries.shape[1]
    tiles, tile, columns = prefix_kv.shape
    groups, count = lax.axis_size("prompt"), lax.axis_size("resp")
    group = lax.axis_index("prompt")
    block = lax.axis_index("resp")
    side = block % 2
    steps = min(count // 2 - 1, (REACH + 1) // 2)
    assert tiles == groups

    def swap(value, first):
        return lax.ppermute(value, "resp", [(r, r ^ 1) for r in range(2 * first, count)])

    def climb(value, step, by):
        pairs = [(r, r + 2 * by) for r in range(2 * (step - by), count - 2 * by)]
        return lax.ppermute(value, "resp", pairs)

    def after(value, *others):
        return lax.optimization_barrier((value, *others))[0]

    mine, theirs = halves(resp_kv[0], side)
    near, far = climb(mine, 1, 1), climb(mine, 2, 2)
    partner = swap(theirs, 0)
    upper = [(r, r + 1) for r in range(0, count, 2)]
    upper = lax.ppermute(after(mine, partner), "resp", upper)
    near2, far2 = climb(partner, 1, 1), climb(partner, 2, 2)
    straight = [mine, partner, near, near2, far, far2]
    swapped, swapped_far = swap(near, 1), swap(far, 2)
    crossed = [theirs, upper, swap(near2, 1), swapped, swap(far2, 2), swapped_far]

    pick = tile_plan[None, :, 0] == jnp.arange(groups, dtype=jnp.int32)[:, None]
    place = jnp.sum(jnp.where(pick, tile_plan[None, :, 1], 0), axis=1, dtype=jnp.int32)
    own_tiles = jnp.sum(
        jnp.where(pick[:, :, None, None], prefix_kv[None], 0).astype(jnp.float32), axis=1
    )
    row = jnp.arange(tile, dtype=jnp.int32)[:, None]
    extra = jnp.where(row == 0, resp_segments[0], place.reshape(groups, 1, 1))
    out_tiles = jnp.concatenate([own_tiles, extra.astype(jnp.float32)], axis=-1)
    out_tiles = jnp.broadcast_to(
        out_tiles.astype(prefix_kv.dtype)[:, None], (groups, count, tile, columns + rows)
    ).reshape(groups * count, tile, columns + rows)
    out_tiles = after(out_tiles, near, far, near2)
    came = lax.all_to_all(
        out_tiles, ("prompt", "resp"), split_axis=0, concat_axis=0, tiled=True
    )
    prefix = came.reshape(-1, columns + rows)

    for step in range(3, steps + 1):
        one = climb(far, step, step - 2)
        two = climb(after(far2, swapped, swapped_far, upper), step, step - 2)
        straight += [one, two]
        crossed += [swap(two, step), swap(one, step)]

    out = None
    for first, pieces in ((side, straight), (1 - side, crossed)):
        meta = jnp.stack([group, block, first * (KVH // 2), prompt_lengths[0]])
        out = attend(meta, resp_segments, queries[0], pieces, prefix, tile, count, out)
    return out[None]


def solution(mesh):
    return jax.shard_map(
        on_device,
        mesh=mesh,
        in_specs=(
            P("prompt", "resp", None),
            P("prompt", "resp", None),
            P("prompt", "resp"),
            P(("prompt", "resp"), None, None),
            P(("prompt", "resp"), None),
            P("prompt"),
        ),
        out_specs=P("prompt", "resp", None),
        check_vma=False,
    )
```

```python
import functools
import math

import jax
import jax.numpy as jnp
from jax import lax
from jax.experimental import pallas as pl
from jax.experimental.pallas import tpu as pltpu
from jax.sharding import PartitionSpec as P

H = 64
KVH = 8
HD = 128
GQ = H // KVH
REACH = 7
SLAB = 2
FILL = -1e30


def halves_kernel(meta_ref, a_ref, b_ref, mine_ref, theirs_ref):
    mine_ref[...] = a_ref[...]
    theirs_ref[...] = b_ref[...]


def halves(kv, side):
    rows, half = kv.shape[0], kv.shape[1] // 4
    shape = (rows, half)
    return pl.pallas_call(
        halves_kernel,
        grid_spec=pltpu.PrefetchScalarGridSpec(
            num_scalar_prefetch=1,
            grid=(2,),
            in_specs=[
                pl.BlockSpec(shape, lambda i, m: (0, 2 * i + m[0])),
                pl.BlockSpec(shape, lambda i, m: (0, 2 * i + 1 - m[0])),
            ],
            out_specs=[pl.BlockSpec(shape, lambda i, m: (0, i))] * 2,
        ),
        out_shape=[jax.ShapeDtypeStruct((rows, 2 * half), kv.dtype)] * 2,
    )(side.reshape(1), kv, kv)


def attend_kernel(pairs, tile, count, fresh, meta_ref, *refs):
    kv_ref, s_ref, top_ref, sems = refs[-4:]
    if fresh:
        seg_ref, q_ref, prefix_ref, *pieces = refs[: 3 + 2 * pairs]
        o_ref, bias_ref, reach_ref, ints_ref, seg_k_ref = refs[3 + 2 * pairs : -4]
    else:
        bias_ref, reach_ref, q_ref, prefix_ref, *pieces = refs[: 4 + 2 * pairs]
        o_ref = refs[-5]
    rows = q_ref.shape[0]
    heads = kv_ref.shape[1] // (2 * HD)
    step = 2 * rows
    prefix_keys = prefix_ref.shape[0]
    group, block, head0, limit = meta_ref[0], meta_ref[1], meta_ref[2], meta_ref[3]
    head = pl.program_id(0)
    scale = math.log2(math.e) / math.sqrt(HD)
    nt = (((1,), (1,)), ((), ()))

    def column(index, width=HD):
        return pl.ds(pl.multiple_of(index * HD, HD), width)

    def masks():
        ints_copy = pltpu.make_async_copy(
            prefix_ref.at[:, pl.ds(2 * KVH * HD, rows)], ints_ref, sems.at[2 * pairs + 2]
        )
        ints_copy.start()
        ints_copy.wait()
        ints = ints_ref[...].astype(jnp.float32)
        seg_k_ref[...] = ints
        part = lax.rem(lax.broadcasted_iota(jnp.int32, ints.shape, 0), tile)
        place = jnp.where(part == 0, pltpu.roll(ints, prefix_keys - 1, 0), ints)
        live = place.astype(jnp.int32) * tile + part < limit
        bias_ref[:, :prefix_keys] = jnp.where(live, 0.0, FILL).T

        own = seg_ref[...].astype(jnp.float32)
        first_key = group * count * tile
        segs = seg_k_ref[pl.ds(pl.multiple_of(first_key, tile), count * tile), :]
        heads_of = lax.rem(lax.broadcasted_iota(jnp.int32, segs.shape, 0), tile) == 0
        earlier = jnp.sum(jnp.where(heads_of & (segs < own[:, :1]), 1.0, 0.0))
        reach_ref[0] = lax.div(block, 2) - lax.div(earlier.astype(jnp.int32), step)

        seg_q = jnp.broadcast_to(own, (rows, rows)).T
        row_pos = block * rows + lax.broadcasted_iota(jnp.int32, (rows, rows), 0)
        lane = lax.broadcasted_iota(jnp.int32, (rows, rows), 1)
        for k in range(pairs):
            for j, first in enumerate((block, block + 1 - 2 * lax.rem(block, 2))):
                key_block = jnp.maximum(first - 2 * k, 0)
                at = pl.multiple_of(first_key + key_block * tile, tile)
                seg_k = seg_k_ref[pl.ds(at, tile), :][:1]
                seen = (seg_k == seg_q) & (key_block * rows + lane <= row_pos)
                at = prefix_keys + (2 * k + j) * rows
                bias_ref[:, at : at + rows] = jnp.where(seen, 0.0, FILL)

    @pl.when(head == 0)
    def _():
        copies = []
        for j, first in enumerate((head0, KVH + head0)):
            copies.append(
                pltpu.make_async_copy(
                    prefix_ref.at[:, column(first, heads * HD)],
                    kv_ref.at[pl.ds(0, prefix_keys), pl.ds(j * heads * HD, heads * HD)],
                    sems.at[j],
                )
            )
        for j, piece in enumerate(pieces):
            at = pl.ds(prefix_keys + j * rows, rows)
            copies.append(pltpu.make_async_copy(piece, kv_ref.at[at], sems.at[2 + j]))
        for copy in copies:
            copy.start()
        if fresh:
            masks()
        for copy in copies:
            copy.wait()

    def body(near):
        steps = prefix_keys // step + near + 1
        values = kv_ref[: steps * step, column(heads + head)]
        values = jnp.concatenate([values, jnp.ones_like(values)], axis=1)

        def score(slab):
            of = range(slab * SLAB, (slab + 1) * SLAB)
            q = jnp.concatenate([q_ref[:, g * HD : (g + 1) * HD] for g in of])
            top = None
            for i in range(steps):
                at = slice(i * step, (i + 1) * step)
                s = lax.dot_general(
                    q, kv_ref[at, column(head)], nt, preferred_element_type=jnp.float32
                )
                s = (s.reshape(SLAB, rows, step) + bias_ref[:, at][None]).reshape(-1, step)
                s_ref[slab % 2, :, at] = s
                high = jnp.maximum(s[:, :rows], s[:, rows:])
                top = high if top is None else jnp.maximum(top, high)
            top = jnp.max(top, axis=1, keepdims=True)
            top_ref[slab % 2] = jnp.broadcast_to(top, (SLAB * rows, HD))

        def weigh(slab):
            top = top_ref[slab % 2]
            weights = [
                jnp.exp2((s_ref[slab % 2, :, i * HD : (i + 1) * HD] - top) * scale).astype(
                    jnp.bfloat16
                )
                for i in range(steps * step // HD)
            ]
            acc = jnp.dot(
                jnp.concatenate(weights, axis=1), values, preferred_element_type=jnp.float32
            )
            out = (acc[:, :HD] / acc[:, HD:]).astype(o_ref.dtype)
            for j in range(SLAB):
                g = slab * SLAB + j
                o_ref[:, g * HD : (g + 1) * HD] = out[j * rows : (j + 1) * rows]

        score(0)
        for slab in range(GQ // SLAB):
            if slab + 1 < GQ // SLAB:
                score(slab + 1)
            weigh(slab)

    for near in range(pairs):
        pl.when(reach_ref[0] == near)(functools.partial(body, near))


def attend(meta, queries, pieces, prefix, tile, count, segments=None, before=None):
    rows = queries.shape[0]
    prefix_keys = prefix.shape[0]
    pairs = len(pieces) // 2
    heads = pieces[0].shape[1] // (2 * HD)
    keys = rows * len(pieces) + prefix_keys
    far = pl.BlockSpec(memory_space=pltpu.HBM)
    whole = pl.BlockSpec((rows, keys), lambda i, m: (0, 0))
    scalar = pl.BlockSpec(memory_space=pltpu.SMEM)
    wide = pl.BlockSpec((rows, GQ * HD), lambda i, m: (0, m[2] + i))
    fresh = before is None
    args = [meta, *([segments] if fresh else before[1:]), queries, prefix, *pieces]
    in_specs = [pl.BlockSpec((1, rows), lambda i, m: (0, 0))] if fresh else [whole, scalar]
    in_specs += [wide, far, *[far] * len(pieces)]
    out_specs = [wide]
    out_shape = [jax.ShapeDtypeStruct(queries.shape, queries.dtype)]
    scratch = []
    aliases = {}
    if fresh:
        out_specs += [whole, scalar]
        out_shape += [
            jax.ShapeDtypeStruct((rows, keys), jnp.float32),
            jax.ShapeDtypeStruct((1,), jnp.int32),
        ]
        scratch = [
            pltpu.VMEM((prefix_keys, rows), queries.dtype),
            pltpu.VMEM((prefix_keys, rows), jnp.float32),
        ]
    else:
        args.append(before[0])
        in_specs.append(far)
        aliases = {len(args) - 1: 0}
    return pl.pallas_call(
        functools.partial(attend_kernel, pairs, tile, count, fresh),
        grid_spec=pltpu.PrefetchScalarGridSpec(
            num_scalar_prefetch=1,
            grid=(heads,),
            in_specs=in_specs,
            out_specs=out_specs,
            scratch_shapes=[
                *scratch,
                pltpu.VMEM((keys, 2 * heads * HD), queries.dtype),
                pltpu.VMEM((2, SLAB * rows, keys), jnp.float32),
                pltpu.VMEM((2, SLAB * rows, HD), jnp.float32),
                pltpu.SemaphoreType.DMA((len(pieces) + 3,)),
            ],
        ),
        out_shape=out_shape,
        input_output_aliases=aliases,
        compiler_params=pltpu.CompilerParams(vmem_limit_bytes=24 * 1024 * 1024),
    )(*args)


def on_device(queries, resp_kv, resp_segments, prefix_kv, tile_plan, prompt_lengths):
    rows = queries.shape[1]
    tiles, tile, columns = prefix_kv.shape
    groups, count = lax.axis_size("prompt"), lax.axis_size("resp")
    group = lax.axis_index("prompt")
    block = lax.axis_index("resp")
    side = block % 2
    steps = min(count // 2 - 1, (REACH + 1) // 2)
    assert tiles == groups

    pick = tile_plan[None, :, 0] == jnp.arange(groups, dtype=jnp.int32)[:, None]
    place = jnp.sum(jnp.where(pick, tile_plan[None, :, 1], 0), axis=1, dtype=jnp.int32)
    own_tiles = jnp.sum(
        jnp.where(pick[:, :, None, None], prefix_kv[None], 0).astype(jnp.float32), axis=1
    )
    row = jnp.arange(tile, dtype=jnp.int32)[:, None]
    extra = jnp.where(row == 0, resp_segments[0], place.reshape(groups, 1, 1))
    out_tiles = jnp.concatenate([own_tiles, extra.astype(jnp.float32)], axis=-1)
    out_tiles = jnp.broadcast_to(
        out_tiles.astype(prefix_kv.dtype)[:, None], (groups, count, tile, columns + rows)
    ).reshape(groups * count, tile, columns + rows)
    came = lax.all_to_all(
        out_tiles, ("prompt", "resp"), split_axis=0, concat_axis=0, tiled=True
    )
    prefix = came.reshape(-1, columns + rows)

    def swap(value, first):
        return lax.ppermute(value, "resp", [(r, r ^ 1) for r in range(2 * first, count)])

    def climb(value, step):
        pairs = [(r, r + 2) for r in range(2 * step - 2, count - 2)]
        return lax.ppermute(value, "resp", pairs)

    def after(value, *others):
        return lax.optimization_barrier((value, *others))[0]

    mine, theirs = halves(resp_kv[0], side)
    partner = swap(theirs, 0)
    upper = [(r, r + 1) for r in range(0, count, 2)]
    upper = lax.ppermute(after(mine, partner), "resp", upper)
    straight, crossed = [mine, partner], [theirs, upper]
    for step in range(1, steps + 1):
        one, two = straight[-2:]
        if step > 2:
            one = after(one, upper, crossed[-3])
            two = after(two, crossed[-4], crossed[-1])
        one, two = climb(one, step), climb(two, step)
        straight += [one, two]
        crossed += [swap(two, step), swap(one, step)]

    def meta(first):
        return jnp.stack([group, block, first * (KVH // 2), prompt_lengths[0]])

    done = attend(
        meta(side), queries[0], straight, prefix, tile, count, segments=resp_segments
    )
    done = attend(meta(1 - side), queries[0], crossed, prefix, tile, count, before=done)
    return done[0][None]


def solution(mesh):
    return jax.shard_map(
        on_device,
        mesh=mesh,
        in_specs=(
            P("prompt", "resp", None),
            P("prompt", "resp", None),
            P("prompt", "resp"),
            P(("prompt", "resp"), None, None),
            P(("prompt", "resp"), None),
            P("prompt"),
        ),
        out_specs=P("prompt", "resp", None),
        check_vma=False,
    )
```

```python
import functools
import math

import jax
import jax.numpy as jnp
from jax import lax
from jax.experimental import pallas as pl
from jax.experimental.pallas import tpu as pltpu
from jax.sharding import PartitionSpec as P

H = 64
KVH = 8
HD = 128
GQ = H // KVH
REACH = 7
SLAB = 2
FILL = -1e30


def halves_kernel(meta_ref, a_ref, b_ref, mine_ref, theirs_ref):
    mine_ref[...] = a_ref[...]
    theirs_ref[...] = b_ref[...]


def halves(kv, side):
    rows, half = kv.shape[0], kv.shape[1] // 4
    shape = (rows, half)
    return pl.pallas_call(
        halves_kernel,
        grid_spec=pltpu.PrefetchScalarGridSpec(
            num_scalar_prefetch=1,
            grid=(2,),
            in_specs=[
                pl.BlockSpec(shape, lambda i, m: (0, 2 * i + m[0])),
                pl.BlockSpec(shape, lambda i, m: (0, 2 * i + 1 - m[0])),
            ],
            out_specs=[pl.BlockSpec(shape, lambda i, m: (0, i))] * 2,
        ),
        out_shape=[jax.ShapeDtypeStruct((rows, 2 * half), kv.dtype)] * 2,
    )(side.reshape(1), kv, kv)


def attend_kernel(pairs, tile, count, fresh, meta_ref, *refs):
    s_ref, top_ref = refs[-2:]
    if fresh:
        seg_ref, ints_ref, q_ref, *inputs = refs[: 5 + 4 * pairs]
        o_ref, bias_ref, reach_ref, seg_k_ref = refs[5 + 4 * pairs : -2]
    else:
        bias_ref, reach_ref, q_ref, *inputs = refs[: 5 + 4 * pairs]
        o_ref = refs[-3]
    pk_ref, pv_ref, *inputs = inputs
    k_refs, v_refs = inputs[: 2 * pairs], inputs[2 * pairs :]
    rows = q_ref.shape[0]
    step = 2 * rows
    prefix_keys = pk_ref.shape[0]
    group, block, limit = meta_ref[0], meta_ref[1], meta_ref[3]
    scale = math.log2(math.e) / math.sqrt(HD)
    nt = (((1,), (1,)), ((), ()))

    def masks():
        ints = ints_ref[...].astype(jnp.float32)
        seg_k_ref[...] = ints
        part = lax.rem(lax.broadcasted_iota(jnp.int32, ints.shape, 0), tile)
        place = jnp.where(part == 0, pltpu.roll(ints, prefix_keys - 1, 0), ints)
        live = place.astype(jnp.int32) * tile + part < limit
        bias_ref[:, :prefix_keys] = jnp.where(live, 0.0, FILL).T

        own = seg_ref[...].astype(jnp.float32)
        first_key = group * count * tile
        segs = seg_k_ref[pl.ds(pl.multiple_of(first_key, tile), count * tile), :]
        heads_of = lax.rem(lax.broadcasted_iota(jnp.int32, segs.shape, 0), tile) == 0
        earlier = jnp.sum(jnp.where(heads_of & (segs < own[:, :1]), 1.0, 0.0))
        reach_ref[0] = lax.div(block, 2) - lax.div(earlier.astype(jnp.int32), step)

        seg_q = jnp.broadcast_to(own, (rows, rows)).T
        row_pos = block * rows + lax.broadcasted_iota(jnp.int32, (rows, rows), 0)
        lane = lax.broadcasted_iota(jnp.int32, (rows, rows), 1)
        for k in range(pairs):
            for j, first in enumerate((block, block + 1 - 2 * lax.rem(block, 2))):
                key_block = jnp.maximum(first - 2 * k, 0)
                at = pl.multiple_of(first_key + key_block * tile, tile)
                seg_k = seg_k_ref[pl.ds(at, tile), :][:1]
                seen = (seg_k == seg_q) & (key_block * rows + lane <= row_pos)
                at = prefix_keys + (2 * k + j) * rows
                bias_ref[:, at : at + rows] = jnp.where(seen, 0.0, FILL)

    if fresh:
        pl.when(pl.program_id(0) == 0)(masks)

    def body(near):
        steps = prefix_keys // step + near + 1
        keys = [pk_ref[at : at + step, :] for at in range(0, prefix_keys, step)]
        for k in range(near + 1):
            keys.append(jnp.concatenate([k_refs[2 * k][...], k_refs[2 * k + 1][...]]))
        values = jnp.concatenate([pv_ref[...]] + [ref[...] for ref in v_refs[: 2 * near + 2]])
        values = jnp.concatenate([values, jnp.ones_like(values)], axis=1)

        def score(slab):
            of = range(slab * SLAB, (slab + 1) * SLAB)
            q = jnp.concatenate([q_ref[:, g * HD : (g + 1) * HD] for g in of])
            top = None
            for i in range(steps):
                at = slice(i * step, (i + 1) * step)
                s = lax.dot_general(q, keys[i], nt, preferred_element_type=jnp.float32)
                s = (s.reshape(SLAB, rows, step) + bias_ref[:, at][None]).reshape(-1, step)
                s_ref[slab % 2, :, at] = s
                high = jnp.maximum(s[:, :rows], s[:, rows:])
                top = high if top is None else jnp.maximum(top, high)
            top = jnp.max(top, axis=1, keepdims=True)
            top_ref[slab % 2] = jnp.broadcast_to(top, (SLAB * rows, HD))

        def weigh(slab):
            top = top_ref[slab % 2]
            weights = [
                jnp.exp2((s_ref[slab % 2, :, i * HD : (i + 1) * HD] - top) * scale).astype(
                    jnp.bfloat16
                )
                for i in range(steps * step // HD)
            ]
            acc = jnp.dot(
                jnp.concatenate(weights, axis=1), values, preferred_element_type=jnp.float32
            )
            out = (acc[:, :HD] / acc[:, HD:]).astype(o_ref.dtype)
            for j in range(SLAB):
                g = slab * SLAB + j
                o_ref[:, g * HD : (g + 1) * HD] = out[j * rows : (j + 1) * rows]

        score(0)
        for slab in range(GQ // SLAB):
            if slab + 1 < GQ // SLAB:
                score(slab + 1)
            weigh(slab)

    for near in range(pairs):
        pl.when(reach_ref[0] == near)(functools.partial(body, near))


def attend(meta, queries, pieces, prefix, tile, count, segments=None, before=None):
    rows = queries.shape[0]
    prefix_keys = prefix.shape[0]
    pairs = len(pieces) // 2
    heads = pieces[0].shape[1] // (2 * HD)
    keys = rows * len(pieces) + prefix_keys
    whole = pl.BlockSpec((rows, keys), lambda i, m: (0, 0))
    scalar = pl.BlockSpec(memory_space=pltpu.SMEM)
    wide = pl.BlockSpec((rows, GQ * HD), lambda i, m: (0, m[2] + i))
    fresh = before is None
    queries, prefix, *pieces = [
        pltpu.with_memory_space_constraint(array, pltpu.HBM) for array in (queries, prefix, *pieces)
    ]
    args = [meta, *([segments, prefix] if fresh else before[1:])]
    args += [queries, prefix, prefix, *pieces, *pieces]
    ints = pl.BlockSpec((prefix_keys, rows), lambda i, m: (0, 2 * KVH))
    in_specs = [pl.BlockSpec((1, rows), lambda i, m: (0, 0)), ints] if fresh else [whole, scalar]
    in_specs += [
        wide,
        pl.BlockSpec((prefix_keys, HD), lambda i, m: (0, m[2] + i)),
        pl.BlockSpec((prefix_keys, HD), lambda i, m: (0, KVH + m[2] + i)),
        *[pl.BlockSpec((rows, HD), lambda i, m: (0, i))] * len(pieces),
        *[pl.BlockSpec((rows, HD), lambda i, m: (0, heads + i))] * len(pieces),
    ]
    out_specs = [wide]
    out_shape = [jax.ShapeDtypeStruct(queries.shape, queries.dtype)]
    scratch = []
    aliases = {}
    if fresh:
        out_specs += [whole, scalar]
        out_shape += [
            jax.ShapeDtypeStruct((rows, keys), jnp.float32),
            jax.ShapeDtypeStruct((1,), jnp.int32),
        ]
        scratch = [pltpu.VMEM((prefix_keys, rows), jnp.float32)]
    else:
        args.append(before[0])
        in_specs.append(pl.BlockSpec(memory_space=pl.ANY))
        aliases = {len(args) - 1: 0}
    return pl.pallas_call(
        functools.partial(attend_kernel, pairs, tile, count, fresh),
        grid_spec=pltpu.PrefetchScalarGridSpec(
            num_scalar_prefetch=1,
            grid=(heads,),
            in_specs=in_specs,
            out_specs=out_specs,
            scratch_shapes=[
                *scratch,
                pltpu.VMEM((2, SLAB * rows, keys), jnp.float32),
                pltpu.VMEM((2, SLAB * rows, HD), jnp.float32),
            ],
        ),
        out_shape=out_shape,
        input_output_aliases=aliases,
        compiler_params=pltpu.CompilerParams(vmem_limit_bytes=24 * 1024 * 1024),
    )(*args)


def on_device(queries, resp_kv, resp_segments, prefix_kv, tile_plan, prompt_lengths):
    rows = queries.shape[1]
    tiles, tile, columns = prefix_kv.shape
    groups, count = lax.axis_size("prompt"), lax.axis_size("resp")
    group = lax.axis_index("prompt")
    block = lax.axis_index("resp")
    side = block % 2
    steps = min(count // 2 - 1, (REACH + 1) // 2)
    assert tiles == groups

    pick = tile_plan[None, :, 0] == jnp.arange(groups, dtype=jnp.int32)[:, None]
    place = jnp.sum(jnp.where(pick, tile_plan[None, :, 1], 0), axis=1, dtype=jnp.int32)
    own_tiles = jnp.sum(
        jnp.where(pick[:, :, None, None], prefix_kv[None], 0).astype(jnp.float32), axis=1
    )
    row = jnp.arange(tile, dtype=jnp.int32)[:, None]
    extra = jnp.where(row == 0, resp_segments[0], place.reshape(groups, 1, 1))
    out_tiles = jnp.concatenate([own_tiles, extra.astype(jnp.float32)], axis=-1)
    out_tiles = jnp.broadcast_to(
        out_tiles.astype(prefix_kv.dtype)[:, None], (groups, count, tile, columns + rows)
    ).reshape(groups * count, tile, columns + rows)
    def swap(value, first):
        return lax.ppermute(value, "resp", [(r, r ^ 1) for r in range(2 * first, count)])

    def climb(value, step):
        pairs = [(r, r + 2) for r in range(2 * step - 2, count - 2)]
        return lax.ppermute(value, "resp", pairs)

    def after(value, *others):
        return lax.optimization_barrier((value, *others))[0]

    mine, theirs = halves(resp_kv[0], side)
    partner = swap(theirs, 0)
    upper = [(r, r + 1) for r in range(0, count, 2)]
    upper = lax.ppermute(after(mine, partner), "resp", upper)
    straight, crossed = [mine, partner], [theirs, upper]
    for step in range(1, steps + 1):
        one, two = straight[-2:]
        if step > 2:
            one = after(one, upper, crossed[-3])
            two = after(two, crossed[-4], crossed[-1])
        one = climb(one, step)
        if step == 1:
            out_tiles = after(out_tiles, one, two)
        two = climb(two, step)
        straight += [one, two]
        crossed += [swap(two, step), swap(one, step)]
    came = lax.all_to_all(
        out_tiles, ("prompt", "resp"), split_axis=0, concat_axis=0, tiled=True
    )
    prefix = came.reshape(-1, columns + rows)

    def meta(first):
        return jnp.stack([group, block, first * (KVH // 2), prompt_lengths[0]])

    done = attend(
        meta(side), queries[0], straight, prefix, tile, count, segments=resp_segments
    )
    done = attend(meta(1 - side), queries[0], crossed, prefix, tile, count, before=done)
    return done[0][None]


def solution(mesh):
    return jax.shard_map(
        on_device,
        mesh=mesh,
        in_specs=(
            P("prompt", "resp", None),
            P("prompt", "resp", None),
            P("prompt", "resp"),
            P(("prompt", "resp"), None, None),
            P(("prompt", "resp"), None),
            P("prompt"),
        ),
        out_specs=P("prompt", "resp", None),
        check_vma=False,
    )
```

```python
import functools
import math

import jax
import jax.numpy as jnp
from jax import lax
from jax.experimental import pallas as pl
from jax.experimental.pallas import tpu as pltpu
from jax.sharding import PartitionSpec as P

H = 64
KVH = 8
HD = 128
GQ = H // KVH
REACH = 7
SLAB = 2
FILL = -1e30


def halves_kernel(meta_ref, a_ref, b_ref, mine_ref, theirs_ref):
    mine_ref[...] = a_ref[...]
    theirs_ref[...] = b_ref[...]


def halves(kv, side):
    rows, half = kv.shape[0], kv.shape[1] // 4
    shape = (rows, half)
    return pl.pallas_call(
        halves_kernel,
        grid_spec=pltpu.PrefetchScalarGridSpec(
            num_scalar_prefetch=1,
            grid=(2,),
            in_specs=[
                pl.BlockSpec(shape, lambda i, m: (0, 2 * i + m[0])),
                pl.BlockSpec(shape, lambda i, m: (0, 2 * i + 1 - m[0])),
            ],
            out_specs=[pl.BlockSpec(shape, lambda i, m: (0, i))] * 2,
        ),
        out_shape=[jax.ShapeDtypeStruct((rows, 2 * half), kv.dtype)] * 2,
    )(side.reshape(1), kv, kv)


def attend_kernel(pairs, tile, count, fresh, meta_ref, *refs):
    s_ref, top_ref = refs[-2:]
    if fresh:
        seg_ref, ints_ref, q_ref, *inputs = refs[: 5 + 4 * pairs]
        o_ref, bias_ref, reach_ref, seg_k_ref = refs[5 + 4 * pairs : -2]
    else:
        bias_ref, reach_ref, q_ref, *inputs = refs[: 5 + 4 * pairs]
        o_ref = refs[-3]
    pk_ref, pv_ref, *inputs = inputs
    k_refs, v_refs = inputs[: 2 * pairs], inputs[2 * pairs :]
    rows = q_ref.shape[0]
    step = 2 * rows
    prefix_keys = pk_ref.shape[0]
    group, block, limit = meta_ref[0], meta_ref[1], meta_ref[3]
    scale = math.log2(math.e) / math.sqrt(HD)
    nt = (((1,), (1,)), ((), ()))

    def masks():
        ints = ints_ref[...].astype(jnp.float32)
        seg_k_ref[...] = ints
        part = lax.rem(lax.broadcasted_iota(jnp.int32, ints.shape, 0), tile)
        place = jnp.where(part == 0, pltpu.roll(ints, prefix_keys - 1, 0), ints)
        live = place.astype(jnp.int32) * tile + part < limit
        bias_ref[:, :prefix_keys] = jnp.where(live, 0.0, FILL).T

        own = seg_ref[...].astype(jnp.float32)
        first_key = group * count * tile
        segs = seg_k_ref[pl.ds(pl.multiple_of(first_key, tile), count * tile), :]
        heads_of = lax.rem(lax.broadcasted_iota(jnp.int32, segs.shape, 0), tile) == 0
        earlier = jnp.sum(jnp.where(heads_of & (segs < own[:, :1]), 1.0, 0.0))
        reach_ref[0] = lax.div(block, 2) - lax.div(earlier.astype(jnp.int32), step)

        seg_q = jnp.broadcast_to(own, (rows, rows)).T
        row_pos = block * rows + lax.broadcasted_iota(jnp.int32, (rows, rows), 0)
        lane = lax.broadcasted_iota(jnp.int32, (rows, rows), 1)
        for k in range(pairs):
            for j, first in enumerate((block, block + 1 - 2 * lax.rem(block, 2))):
                key_block = jnp.maximum(first - 2 * k, 0)
                at = pl.multiple_of(first_key + key_block * tile, tile)
                seg_k = seg_k_ref[pl.ds(at, tile), :][:1]
                seen = (seg_k == seg_q) & (key_block * rows + lane <= row_pos)
                at = prefix_keys + (2 * k + j) * rows
                bias_ref[:, at : at + rows] = jnp.where(seen, 0.0, FILL)

    if fresh:
        pl.when(pl.program_id(0) == 0)(masks)

    def body(near):
        steps = prefix_keys // step + near + 1
        keys = [pk_ref[at : at + step, :] for at in range(0, prefix_keys, step)]
        for k in range(near + 1):
            keys.append(jnp.concatenate([k_refs[2 * k][...], k_refs[2 * k + 1][...]]))
        values = jnp.concatenate([pv_ref[...]] + [ref[...] for ref in v_refs[: 2 * near + 2]])
        values = jnp.concatenate([values, jnp.ones_like(values)], axis=1)

        def score(slab):
            of = range(slab * SLAB, (slab + 1) * SLAB)
            q = jnp.concatenate([q_ref[:, g * HD : (g + 1) * HD] for g in of])
            top = None
            for i in range(steps):
                at = slice(i * step, (i + 1) * step)
                s = lax.dot_general(q, keys[i], nt, preferred_element_type=jnp.float32)
                s = (s.reshape(SLAB, rows, step) + bias_ref[:, at][None]).reshape(-1, step)
                s_ref[slab % 2, :, at] = s
                high = jnp.maximum(s[:, :rows], s[:, rows:])
                top = high if top is None else jnp.maximum(top, high)
            top = jnp.max(top, axis=1, keepdims=True)
            top_ref[slab % 2] = jnp.broadcast_to(top, (SLAB * rows, HD))

        def weigh(slab):
            top = top_ref[slab % 2]
            weights = [
                jnp.exp2((s_ref[slab % 2, :, i * HD : (i + 1) * HD] - top) * scale).astype(
                    jnp.bfloat16
                )
                for i in range(steps * step // HD)
            ]
            acc = jnp.dot(
                jnp.concatenate(weights, axis=1), values, preferred_element_type=jnp.float32
            )
            out = (acc[:, :HD] / acc[:, HD:]).astype(o_ref.dtype)
            for j in range(SLAB):
                g = slab * SLAB + j
                o_ref[:, g * HD : (g + 1) * HD] = out[j * rows : (j + 1) * rows]

        score(0)
        for slab in range(GQ // SLAB):
            if slab + 1 < GQ // SLAB:
                score(slab + 1)
            weigh(slab)

    for near in range(pairs):
        pl.when(reach_ref[0] == near)(functools.partial(body, near))


def attend(meta, queries, pieces, prefix, tile, count, segments=None, before=None):
    rows = queries.shape[0]
    prefix_keys = prefix.shape[0]
    pairs = len(pieces) // 2
    heads = pieces[0].shape[1] // (2 * HD)
    keys = rows * len(pieces) + prefix_keys
    whole = pl.BlockSpec((rows, keys), lambda i, m: (0, 0))
    scalar = pl.BlockSpec(memory_space=pltpu.SMEM)
    wide = pl.BlockSpec((rows, GQ * HD), lambda i, m: (0, m[2] + i))
    fresh = before is None
    queries, prefix, *pieces = [
        pltpu.with_memory_space_constraint(array, pltpu.HBM) for array in (queries, prefix, *pieces)
    ]
    args = [meta, *([segments, prefix] if fresh else before[1:])]
    args += [queries, prefix, prefix, *pieces, *pieces]
    ints = pl.BlockSpec((prefix_keys, rows), lambda i, m: (0, 2 * heads))
    in_specs = [pl.BlockSpec((1, rows), lambda i, m: (0, 0)), ints] if fresh else [whole, scalar]
    in_specs += [
        wide,
        pl.BlockSpec((prefix_keys, HD), lambda i, m: (0, i)),
        pl.BlockSpec((prefix_keys, HD), lambda i, m: (0, heads + i)),
        *[pl.BlockSpec((rows, HD), lambda i, m: (0, i))] * len(pieces),
        *[pl.BlockSpec((rows, HD), lambda i, m: (0, heads + i))] * len(pieces),
    ]
    out_specs = [wide]
    out_shape = [jax.ShapeDtypeStruct(queries.shape, queries.dtype)]
    scratch = []
    aliases = {}
    if fresh:
        out_specs += [whole, scalar]
        out_shape += [
            jax.ShapeDtypeStruct((rows, keys), jnp.float32),
            jax.ShapeDtypeStruct((1,), jnp.int32),
        ]
        scratch = [pltpu.VMEM((prefix_keys, rows), jnp.float32)]
    else:
        args.append(before[0])
        in_specs.append(pl.BlockSpec(memory_space=pl.ANY))
        aliases = {len(args) - 1: 0}
    return pl.pallas_call(
        functools.partial(attend_kernel, pairs, tile, count, fresh),
        grid_spec=pltpu.PrefetchScalarGridSpec(
            num_scalar_prefetch=1,
            grid=(heads,),
            in_specs=in_specs,
            out_specs=out_specs,
            scratch_shapes=[
                *scratch,
                pltpu.VMEM((2, SLAB * rows, keys), jnp.float32),
                pltpu.VMEM((2, SLAB * rows, HD), jnp.float32),
            ],
        ),
        out_shape=out_shape,
        input_output_aliases=aliases,
        compiler_params=pltpu.CompilerParams(vmem_limit_bytes=24 * 1024 * 1024),
    )(*args)


def on_device(queries, resp_kv, resp_segments, prefix_kv, tile_plan, prompt_lengths):
    rows = queries.shape[1]
    tiles, tile, columns = prefix_kv.shape
    groups, count = lax.axis_size("prompt"), lax.axis_size("resp")
    group = lax.axis_index("prompt")
    block = lax.axis_index("resp")
    side = block % 2
    steps = min(count // 2 - 1, (REACH + 1) // 2)
    assert tiles == groups

    pick = tile_plan[None, :, 0] == jnp.arange(groups, dtype=jnp.int32)[:, None]
    place = jnp.sum(jnp.where(pick, tile_plan[None, :, 1], 0), axis=1, dtype=jnp.int32)
    own_tiles = jnp.sum(
        jnp.where(pick[:, :, None, None], prefix_kv[None], 0).astype(jnp.float32), axis=1
    )
    own_tiles = own_tiles.astype(prefix_kv.dtype)
    half = columns // 4
    row = jnp.arange(tile, dtype=jnp.int32)[:, None]
    extra = jnp.where(row == 0, resp_segments[0], place.reshape(groups, 1, 1))
    extra = extra.astype(prefix_kv.dtype)
    out_tiles = [
        jnp.concatenate(
            [own_tiles[..., at : at + half], own_tiles[..., at + 2 * half :][..., :half], extra],
            axis=-1,
        )
        for at in (0, half)
    ]
    out_tiles = jnp.broadcast_to(
        jnp.stack(out_tiles, axis=1)[:, None], (groups, count // 2, 2, tile, 2 * half + rows)
    ).reshape(groups * count, tile, 2 * half + rows)
    def swap(value, first):
        return lax.ppermute(value, "resp", [(r, r ^ 1) for r in range(2 * first, count)])

    def climb(value, step):
        pairs = [(r, r + 2) for r in range(2 * step - 2, count - 2)]
        return lax.ppermute(value, "resp", pairs)

    def after(value, *others):
        return lax.optimization_barrier((value, *others))[0]

    mine, theirs = halves(resp_kv[0], side)
    partner = swap(theirs, 0)
    upper = [(r, r + 1) for r in range(0, count, 2)]
    upper = lax.ppermute(after(mine, partner), "resp", upper)
    straight, crossed = [mine, partner], [theirs, upper]
    for step in range(1, steps + 1):
        one, two = straight[-2:]
        one = climb(one, step)
        if step == 1:
            out_tiles = after(out_tiles, one, two)
            prefix = lax.all_to_all(
                out_tiles, ("prompt", "resp"), split_axis=0, concat_axis=0, tiled=True
            ).reshape(-1, 2 * half + rows)
            prefix_crossed = swap(prefix, 0)
        if step > 2:
            two = after(two, upper, prefix_crossed, *crossed[-4:-2], crossed[-1])
        two = climb(two, step)
        straight += [one, two]
        crossed += [swap(two, step), swap(one, step)]

    def meta(first):
        return jnp.stack([group, block, first * (KVH // 2), prompt_lengths[0]])

    done = attend(
        meta(side), queries[0], straight, prefix, tile, count, segments=resp_segments
    )
    done = attend(meta(1 - side), queries[0], crossed, prefix_crossed, tile, count, before=done)
    return done[0][None]


def solution(mesh):
    return jax.shard_map(
        on_device,
        mesh=mesh,
        in_specs=(
            P("prompt", "resp", None),
            P("prompt", "resp", None),
            P("prompt", "resp"),
            P(("prompt", "resp"), None, None),
            P(("prompt", "resp"), None),
            P("prompt"),
        ),
        out_specs=P("prompt", "resp", None),
        check_vma=False,
    )
```

```python
import functools
import math

import jax
import jax.numpy as jnp
from jax import lax
from jax.experimental import pallas as pl
from jax.experimental.pallas import tpu as pltpu
from jax.sharding import PartitionSpec as P

H = 64
KVH = 8
HD = 128
GQ = H // KVH
REACH = 7
SLAB = 2
FILL = -1e30


def halves_kernel(meta_ref, a_ref, b_ref, mine_ref, theirs_ref):
    mine_ref[...] = a_ref[...]
    theirs_ref[...] = b_ref[...]


def halves(kv, side):
    rows, half = kv.shape[0], kv.shape[1] // 4
    shape = (rows, half)
    return pl.pallas_call(
        halves_kernel,
        grid_spec=pltpu.PrefetchScalarGridSpec(
            num_scalar_prefetch=1,
            grid=(2,),
            in_specs=[
                pl.BlockSpec(shape, lambda i, m: (0, 2 * i + m[0])),
                pl.BlockSpec(shape, lambda i, m: (0, 2 * i + 1 - m[0])),
            ],
            out_specs=[pl.BlockSpec(shape, lambda i, m: (0, i))] * 2,
        ),
        out_shape=[jax.ShapeDtypeStruct((rows, 2 * half), kv.dtype)] * 2,
    )(side.reshape(1), kv, kv)


def attend_kernel(pairs, parts, tile, tiles, fresh, meta_ref, *refs):
    s_ref, top_ref = refs[-2:]
    inputs = 2 * parts + 4 * pairs
    if fresh:
        seg_ref, *ints_refs = refs[: 1 + parts]
        q_ref, *inputs = refs[1 + parts : 2 + parts + inputs]
        o_ref, bias_ref, reach_ref = refs[-5:-2]
    else:
        bias_ref, reach_ref, q_ref, *inputs = refs[: 3 + inputs]
        o_ref = refs[-3]
    pk_refs, pv_refs = inputs[:parts], inputs[parts : 2 * parts]
    k_refs, v_refs = inputs[2 * parts :][: 2 * pairs], inputs[2 * parts + 2 * pairs :]
    rows = q_ref.shape[0]
    step = 2 * rows
    span = pk_refs[0].shape[0]
    prefix_keys = parts * span
    block, limit = meta_ref[0], meta_ref[2]
    scale = math.log2(math.e) / math.sqrt(HD)
    nt = (((1,), (1,)), ((), ()))

    def masks():
        ints = jnp.concatenate([ref[...].astype(jnp.float32) for ref in ints_refs])
        row = lax.broadcasted_iota(jnp.int32, ints.shape, 0)
        part = lax.rem(row, tile)
        place = jnp.where(part == 0, pltpu.roll(ints, prefix_keys - 1, 0), ints)
        live = place.astype(jnp.int32) * tile + part < limit
        bias_ref[:, :prefix_keys] = jnp.where(live, 0.0, FILL).T

        own = seg_ref[...].astype(jnp.float32)
        has_segs = lax.rem(row, tiles * tile) == 0
        earlier = jnp.sum(jnp.where(has_segs & (ints < own[:, :1]), 1.0, 0.0))
        reach_ref[0] = lax.div(block, 2) - lax.div(earlier.astype(jnp.int32), step)

        seg_q = jnp.broadcast_to(own, (rows, rows)).T
        row_pos = block * rows + lax.broadcasted_iota(jnp.int32, (rows, rows), 0)
        lane = lax.broadcasted_iota(jnp.int32, (rows, rows), 1)
        for k in range(pairs):
            for j, first in enumerate((block, block + 1 - 2 * lax.rem(block, 2))):
                at = (2 * k + j) * tiles * tile
                seen = (ints[at : at + 1] == seg_q) & ((first - 2 * k) * rows + lane <= row_pos)
                at = prefix_keys + (2 * k + j) * rows
                bias_ref[:, at : at + rows] = jnp.where(seen, 0.0, FILL)

    if fresh:
        pl.when(pl.program_id(0) == 0)(masks)

    def body(near):
        steps = prefix_keys // step + near + 1
        each = step // span
        keys = [
            jnp.concatenate([ref[...] for ref in pk_refs[at : at + each]])
            for at in range(0, parts, each)
        ]
        for k in range(near + 1):
            keys.append(jnp.concatenate([k_refs[2 * k][...], k_refs[2 * k + 1][...]]))
        values = jnp.concatenate([ref[...] for ref in (*pv_refs, *v_refs[: 2 * near + 2])])
        values = jnp.concatenate([values, jnp.ones_like(values)], axis=1)

        def score(slab):
            of = range(slab * SLAB, (slab + 1) * SLAB)
            q = jnp.concatenate([q_ref[:, g * HD : (g + 1) * HD] for g in of])
            top = None
            for i in range(steps):
                at = slice(i * step, (i + 1) * step)
                s = lax.dot_general(q, keys[i], nt, preferred_element_type=jnp.float32)
                s = (s.reshape(SLAB, rows, step) + bias_ref[:, at][None]).reshape(-1, step)
                s_ref[slab % 2, :, at] = s
                high = jnp.maximum(s[:, :rows], s[:, rows:])
                top = high if top is None else jnp.maximum(top, high)
            top = jnp.max(top, axis=1, keepdims=True)
            top_ref[slab % 2] = jnp.broadcast_to(top, (SLAB * rows, HD))

        def weigh(slab):
            top = top_ref[slab % 2]
            weights = [
                jnp.exp2((s_ref[slab % 2, :, i * HD : (i + 1) * HD] - top) * scale).astype(
                    jnp.bfloat16
                )
                for i in range(steps * step // HD)
            ]
            acc = jnp.dot(
                jnp.concatenate(weights, axis=1), values, preferred_element_type=jnp.float32
            )
            out = (acc[:, :HD] / acc[:, HD:]).astype(o_ref.dtype)
            for j in range(SLAB):
                g = slab * SLAB + j
                o_ref[:, g * HD : (g + 1) * HD] = out[j * rows : (j + 1) * rows]

        score(0)
        for slab in range(GQ // SLAB):
            if slab + 1 < GQ // SLAB:
                score(slab + 1)
            weigh(slab)

    for near in range(pairs):
        pl.when(reach_ref[0] == near)(functools.partial(body, near))


def attend(meta, queries, pieces, prefix, tile, tiles, segments=None, before=None):
    rows = queries.shape[0]
    span = prefix[0].shape[0]
    pairs, parts = len(pieces) // 2, len(prefix)
    heads = pieces[0].shape[1] // (2 * HD)
    keys = rows * len(pieces) + span * parts
    whole = pl.BlockSpec((rows, keys), lambda i, m: (0, 0))
    scalar = pl.BlockSpec(memory_space=pltpu.SMEM)
    wide = pl.BlockSpec((rows, GQ * HD), lambda i, m: (0, m[1] + i))
    fresh = before is None
    queries, *arrays = [
        pltpu.with_memory_space_constraint(array, pltpu.HBM)
        for array in (queries, *prefix, *pieces)
    ]
    prefix, pieces = arrays[:parts], arrays[parts:]
    args = [meta, *([segments, *prefix] if fresh else before[1:])]
    args += [queries, *prefix, *prefix, *pieces, *pieces]
    if fresh:
        ints = pl.BlockSpec((span, rows), lambda i, m: (0, 2 * KVH))
        in_specs = [pl.BlockSpec((1, rows), lambda i, m: (0, 0)), *[ints] * parts]
    else:
        in_specs = [whole, scalar]
    in_specs += [
        wide,
        *[pl.BlockSpec((span, HD), lambda i, m: (0, m[1] + i))] * parts,
        *[pl.BlockSpec((span, HD), lambda i, m: (0, KVH + m[1] + i))] * parts,
        *[pl.BlockSpec((rows, HD), lambda i, m: (0, i))] * len(pieces),
        *[pl.BlockSpec((rows, HD), lambda i, m: (0, heads + i))] * len(pieces),
    ]
    out_specs = [wide]
    out_shape = [jax.ShapeDtypeStruct(queries.shape, queries.dtype)]
    aliases = {}
    if fresh:
        out_specs += [whole, scalar]
        out_shape += [
            jax.ShapeDtypeStruct((rows, keys), jnp.float32),
            jax.ShapeDtypeStruct((1,), jnp.int32),
        ]
    else:
        args.append(before[0])
        in_specs.append(pl.BlockSpec(memory_space=pl.ANY))
        aliases = {len(args) - 1: 0}
    return pl.pallas_call(
        functools.partial(attend_kernel, pairs, parts, tile, tiles, fresh),
        grid_spec=pltpu.PrefetchScalarGridSpec(
            num_scalar_prefetch=1,
            grid=(heads,),
            in_specs=in_specs,
            out_specs=out_specs,
            scratch_shapes=[
                pltpu.VMEM((2, SLAB * rows, keys), jnp.float32),
                pltpu.VMEM((2, SLAB * rows, HD), jnp.float32),
            ],
        ),
        out_shape=out_shape,
        input_output_aliases=aliases,
        compiler_params=pltpu.CompilerParams(vmem_limit_bytes=24 * 1024 * 1024),
    )(*args)


def on_device(queries, resp_kv, resp_segments, prefix_kv, tile_plan, prompt_lengths):
    rows = queries.shape[1]
    tiles, tile, columns = prefix_kv.shape
    groups, count = lax.axis_size("prompt"), lax.axis_size("resp")
    group = lax.axis_index("prompt")
    block = lax.axis_index("resp")
    side = block % 2
    steps = min(count // 2 - 1, (REACH + 1) // 2)
    assert tiles == groups

    def swap(value, first):
        return lax.ppermute(value, "resp", [(r, r ^ 1) for r in range(2 * first, count)])

    def climb(value, step):
        pairs = [(r, r + 2) for r in range(2 * step - 2, count - 2)]
        return lax.ppermute(value, "resp", pairs)

    def shift(value, axis, by):
        size = lax.axis_size(axis)
        return lax.ppermute(value, axis, [(r, (r + by) % size) for r in range(size)])

    def after(value, *others):
        return lax.optimization_barrier((value, *others))[0]

    mine, theirs = halves(resp_kv[0], side)
    partner = swap(theirs, 0)
    upper = [(r, r + 1) for r in range(0, count, 2)]
    upper = lax.ppermute(after(mine, partner), "resp", upper)
    straight, crossed = [mine, partner], [theirs, upper]
    for step in range(1, steps + 1):
        one, two = straight[-2:]
        if step > 2:
            one, two = after(one, crossed[-3]), after(two, crossed[-4], upper)
        one, two = climb(one, step), climb(two, step)
        straight += [one, two]
        crossed += [swap(two, step), swap(one, step)]

    owners = (group + jnp.arange(groups, dtype=jnp.int32)) % groups
    pick = tile_plan[None, :, 0] == owners[:, None]
    place = jnp.sum(jnp.where(pick, tile_plan[None, :, 1], 0), axis=1, dtype=jnp.int32)
    own_tiles = jnp.sum(
        jnp.where(pick[:, :, None, None], prefix_kv[None], 0).astype(jnp.float32), axis=1
    )
    row = jnp.arange(tile, dtype=jnp.int32)[:, None]
    extra = jnp.where(row == 0, resp_segments[0], place.reshape(groups, 1, 1))
    own_tiles = jnp.concatenate([own_tiles, extra.astype(jnp.float32)], axis=-1)
    own_tiles = own_tiles.astype(prefix_kv.dtype)
    came = [own_tiles[0]] + [shift(own_tiles[by], "prompt", by) for by in range(1, groups)]
    came = jnp.concatenate(came)
    prefix = [jnp.concatenate([came, swap(came, 0)])]
    prefix += [shift(prefix[0], "resp", 2 * by) for by in range(1, count // 2)]

    def meta(first):
        return jnp.stack([block, first * (KVH // 2), prompt_lengths[0]])

    done = attend(
        meta(side), queries[0], straight, prefix, tile, tiles, segments=resp_segments
    )
    done = attend(meta(1 - side), queries[0], crossed, prefix, tile, tiles, before=done)
    return done[0][None]


def solution(mesh):
    return jax.shard_map(
        on_device,
        mesh=mesh,
        in_specs=(
            P("prompt", "resp", None),
            P("prompt", "resp", None),
            P("prompt", "resp"),
            P(("prompt", "resp"), None, None),
            P(("prompt", "resp"), None),
            P("prompt"),
        ),
        out_specs=P("prompt", "resp", None),
        check_vma=False,
    )
```

```python
import functools
import math

import jax
import jax.numpy as jnp
from jax import lax
from jax.experimental import pallas as pl
from jax.experimental.pallas import tpu as pltpu
from jax.sharding import PartitionSpec as P

H = 64
KVH = 8
HD = 128
GQ = H // KVH
REACH = 7
SLAB = 2
BOTH = 2
FILL = -1e30


def halves_kernel(meta_ref, a_ref, b_ref, mine_ref, theirs_ref):
    mine_ref[...] = a_ref[...]
    theirs_ref[...] = b_ref[...]


def halves(kv, side):
    rows, half = kv.shape[0], kv.shape[1] // 4
    shape = (rows, half)
    return pl.pallas_call(
        halves_kernel,
        grid_spec=pltpu.PrefetchScalarGridSpec(
            num_scalar_prefetch=1,
            grid=(2,),
            in_specs=[
                pl.BlockSpec(shape, lambda i, m: (0, 2 * i + m[0])),
                pl.BlockSpec(shape, lambda i, m: (0, 2 * i + 1 - m[0])),
            ],
            out_specs=[pl.BlockSpec(shape, lambda i, m: (0, i))] * 2,
        ),
        out_shape=[jax.ShapeDtypeStruct((rows, 2 * half), kv.dtype)] * 2,
    )(side.reshape(1), kv, kv)


def attend_kernel(pairs, tile, tiles, fresh, meta_ref, *refs):
    s_ref, top_ref = refs[-2:]
    if fresh:
        seg_ref, ints_ref, q_ref, *inputs = refs[: 5 + 4 * pairs]
        o_ref, bias_ref, reach_ref, seg_k_ref = refs[5 + 4 * pairs : -2]
    else:
        bias_ref, reach_ref, q_ref, *inputs = refs[: 5 + 4 * pairs]
        o_ref = refs[-3]
    pk_ref, pv_ref, *inputs = inputs
    k_refs, v_refs = inputs[: 2 * pairs], inputs[2 * pairs :]
    rows = q_ref.shape[0]
    step = 2 * rows
    prefix_keys = pk_ref.shape[0]
    block, limit = meta_ref[0], meta_ref[2]
    scale = math.log2(math.e) / math.sqrt(HD)
    nt = (((1,), (1,)), ((), ()))

    def masks():
        ints = ints_ref[...].astype(jnp.float32)
        seg_k_ref[...] = ints
        row = lax.broadcasted_iota(jnp.int32, ints.shape, 0)
        part = lax.rem(row, tile)
        place = jnp.where(part == 0, pltpu.roll(ints, prefix_keys - 1, 0), ints)
        live = place.astype(jnp.int32) * tile + part < limit
        bias_ref[:, :prefix_keys] = jnp.where(live, 0.0, FILL).T

        own = seg_ref[...].astype(jnp.float32)
        has_segs = lax.rem(row, tiles * tile) == 0
        earlier = jnp.sum(jnp.where(has_segs & (ints < own[:, :1]), 1.0, 0.0))
        own_pair = lax.div(block, 2)
        reach_ref[0] = own_pair - lax.div(earlier.astype(jnp.int32), step)

        seg_q = jnp.broadcast_to(own, (rows, rows)).T
        row_pos = block * rows + lax.broadcasted_iota(jnp.int32, (rows, rows), 0)
        lane = lax.broadcasted_iota(jnp.int32, (rows, rows), 1)
        for k in range(pairs):
            pair = jnp.maximum(own_pair - k, 0)
            for j, first in enumerate((block, block + 1 - 2 * lax.rem(block, 2))):
                at = pl.multiple_of((2 * pair + j) * tiles * tile, tile)
                seg_k = seg_k_ref[pl.ds(at, tile), :][:1]
                seen = (seg_k == seg_q) & ((first - 2 * k) * rows + lane <= row_pos)
                at = prefix_keys + (2 * k + j) * rows
                bias_ref[:, at : at + rows] = jnp.where(seen, 0.0, FILL)

    if fresh:
        pl.when(pl.program_id(0) == 0)(masks)

    def body(near):
        steps = prefix_keys // step + near + 1

        def score(slab):
            head = pl.ds(slab // (GQ // SLAB) * HD, HD)
            of = range(slab * SLAB, (slab + 1) * SLAB)
            q = jnp.concatenate([q_ref[:, g * HD : (g + 1) * HD] for g in of])
            top = None
            for i in range(steps):
                at = slice(i * step, (i + 1) * step)
                if i < prefix_keys // step:
                    keys = pk_ref[at, head]
                else:
                    j = 2 * (i - prefix_keys // step)
                    keys = jnp.concatenate([ref[:, head] for ref in k_refs[j : j + 2]])
                s = lax.dot_general(q, keys, nt, preferred_element_type=jnp.float32)
                s = (s.reshape(SLAB, rows, step) + bias_ref[:, at][None]).reshape(-1, step)
                s_ref[slab % 2, :, at] = s
                high = jnp.maximum(s[:, :rows], s[:, rows:])
                top = high if top is None else jnp.maximum(top, high)
            top = jnp.max(top, axis=1, keepdims=True)
            top_ref[slab % 2] = jnp.broadcast_to(top, (SLAB * rows, HD))

        def weigh(slab):
            head = pl.ds(slab // (GQ // SLAB) * HD, HD)
            values = [ref[:, head] for ref in (pv_ref, *v_refs[: 2 * near + 2])]
            values = jnp.concatenate(values)
            values = jnp.concatenate([values, jnp.ones_like(values)], axis=1)
            top = top_ref[slab % 2]
            weights = [
                jnp.exp2((s_ref[slab % 2, :, i * HD : (i + 1) * HD] - top) * scale).astype(
                    jnp.bfloat16
                )
                for i in range(steps * step // HD)
            ]
            acc = jnp.dot(
                jnp.concatenate(weights, axis=1), values, preferred_element_type=jnp.float32
            )
            out = (acc[:, :HD] / acc[:, HD:]).astype(o_ref.dtype)
            for j in range(SLAB):
                g = slab * SLAB + j
                o_ref[:, g * HD : (g + 1) * HD] = out[j * rows : (j + 1) * rows]

        slabs = BOTH * GQ // SLAB
        score(0)
        for slab in range(slabs):
            if slab + 1 < slabs:
                score(slab + 1)
            weigh(slab)

    for near in range(pairs):
        pl.when(reach_ref[0] == near)(functools.partial(body, near))


def attend(meta, queries, pieces, prefix, tile, tiles, segments=None, before=None):
    rows = queries.shape[0]
    prefix_keys = prefix.shape[0]
    pairs = len(pieces) // 2
    pieces, places = zip(*[piece if isinstance(piece, tuple) else (piece, 0) for piece in pieces])
    heads = pieces[0].shape[1] // (2 * HD)
    blocks = heads // BOTH
    keys = rows * len(pieces) + prefix_keys
    whole = pl.BlockSpec((rows, keys), lambda i, m: (0, 0))
    scalar = pl.BlockSpec(memory_space=pltpu.SMEM)
    wide = pl.BlockSpec((rows, BOTH * GQ * HD), lambda i, m: (0, m[1] + i))
    fresh = before is None
    queries, prefix, *pieces = [
        pltpu.with_memory_space_constraint(array, pltpu.HBM) for array in (queries, prefix, *pieces)
    ]
    args = [meta, *([segments, prefix] if fresh else before[1:])]
    args += [queries, prefix, prefix, *pieces, *pieces]
    ints = pl.BlockSpec((prefix_keys, rows), lambda i, m: (0, 2 * KVH))
    in_specs = [pl.BlockSpec((1, rows), lambda i, m: (0, 0)), ints] if fresh else [whole, scalar]
    in_specs += [
        wide,
        pl.BlockSpec((prefix_keys, BOTH * HD), lambda i, m: (0, m[1] + i)),
        pl.BlockSpec((prefix_keys, BOTH * HD), lambda i, m: (0, KVH // BOTH + m[1] + i)),
        *[pl.BlockSpec((rows, BOTH * HD), lambda i, m, at=at: (at, i)) for at in places],
        *[pl.BlockSpec((rows, BOTH * HD), lambda i, m, at=at: (at, blocks + i)) for at in places],
    ]
    out_specs = [wide]
    scratch = []
    out_shape = [jax.ShapeDtypeStruct(queries.shape, queries.dtype)]
    aliases = {}
    if fresh:
        out_specs += [whole, scalar]
        out_shape += [
            jax.ShapeDtypeStruct((rows, keys), jnp.float32),
            jax.ShapeDtypeStruct((1,), jnp.int32),
        ]
        scratch = [pltpu.VMEM((prefix_keys, rows), jnp.float32)]
    else:
        args.append(before[0])
        in_specs.append(pl.BlockSpec(memory_space=pl.ANY))
        aliases = {len(args) - 1: 0}
    return pl.pallas_call(
        functools.partial(attend_kernel, pairs, tile, tiles, fresh),
        grid_spec=pltpu.PrefetchScalarGridSpec(
            num_scalar_prefetch=1,
            grid=(blocks,),
            in_specs=in_specs,
            out_specs=out_specs,
            scratch_shapes=[
                *scratch,
                pltpu.VMEM((2, SLAB * rows, keys), jnp.float32),
                pltpu.VMEM((2, SLAB * rows, HD), jnp.float32),
            ],
        ),
        out_shape=out_shape,
        input_output_aliases=aliases,
        compiler_params=pltpu.CompilerParams(vmem_limit_bytes=24 * 1024 * 1024),
    )(*args)


def on_device(queries, resp_kv, resp_segments, prefix_kv, tile_plan, prompt_lengths):
    rows = queries.shape[1]
    tiles, tile, columns = prefix_kv.shape
    groups, count = lax.axis_size("prompt"), lax.axis_size("resp")
    group = lax.axis_index("prompt")
    block = lax.axis_index("resp")
    side = block % 2
    steps = min(count // 2 - 1, (REACH + 1) // 2)
    assert tiles == groups

    def swap(value, first):
        return lax.ppermute(value, "resp", [(r, r ^ 1) for r in range(2 * first, count)])

    def climb(value, step):
        pairs = [(r, r + 2) for r in range(2 * step - 2, count - 2)]
        return lax.ppermute(value, "resp", pairs)

    def shift(value, axis, by):
        size = lax.axis_size(axis)
        return lax.ppermute(value, axis, [(r, (r + by) % size) for r in range(size)])

    def after(value, *others):
        return lax.optimization_barrier((value, *others))[0]

    mine, theirs = halves(resp_kv[0], side)
    partner = swap(theirs, 0)
    upper = [(r, r + 1) for r in range(0, count, 2)]
    upper = lax.ppermute(after(mine, partner), "resp", upper)
    straight, crossed = [mine, partner], [theirs, upper]
    for step in range(1, steps + 1):
        one, two = straight[-2:]
        if step > 2:
            two = after(two, crossed[2][0], upper)
        one, two = climb(one, step), climb(two, step)
        straight += [one, two]
        if step < steps:
            both = swap(jnp.concatenate([two, one]), step)
            crossed += [(both, 0), (both, 1)]
        else:
            crossed += [swap(two, step), swap(one, step)]

    owners = (group + jnp.arange(groups, dtype=jnp.int32)) % groups
    pick = tile_plan[None, :, 0] == owners[:, None]
    place = jnp.sum(jnp.where(pick, tile_plan[None, :, 1], 0), axis=1, dtype=jnp.int32)
    own_tiles = jnp.sum(
        jnp.where(pick[:, :, None, None], prefix_kv[None], 0).astype(jnp.float32), axis=1
    )
    row = jnp.arange(tile, dtype=jnp.int32)[:, None]
    extra = jnp.where(row == 0, resp_segments[0], place.reshape(groups, 1, 1))
    own_tiles = jnp.concatenate([own_tiles, extra.astype(jnp.float32)], axis=-1)
    own_tiles = own_tiles.astype(prefix_kv.dtype)
    came = [own_tiles[0]] + [shift(own_tiles[by], "prompt", by) for by in range(1, groups)]
    came = jnp.concatenate(came)
    came = jnp.concatenate([came, swap(came, 0)])
    came = jnp.broadcast_to(after(came, *straight[2:4])[None], (count // 2, *came.shape))
    columns_of = [list(range(first, count, 2)) for first in range(2)]
    prefix = lax.all_to_all(
        came, "resp", split_axis=0, concat_axis=0, axis_index_groups=columns_of, tiled=True
    ).reshape(-1, columns + rows)

    def meta(first):
        return jnp.stack([block, first * (KVH // 2 // BOTH), prompt_lengths[0]])

    done = attend(
        meta(side), queries[0], straight, prefix, tile, tiles, segments=resp_segments
    )
    done = attend(meta(1 - side), queries[0], crossed, prefix, tile, tiles, before=done)
    return done[0][None]


def solution(mesh):
    return jax.shard_map(
        on_device,
        mesh=mesh,
        in_specs=(
            P("prompt", "resp", None),
            P("prompt", "resp", None),
            P("prompt", "resp"),
            P(("prompt", "resp"), None, None),
            P(("prompt", "resp"), None),
            P("prompt"),
        ),
        out_specs=P("prompt", "resp", None),
        check_vma=False,
    )
```

```python
import functools
import math

import jax
import jax.numpy as jnp
from jax import lax
from jax.experimental import pallas as pl
from jax.experimental.pallas import tpu as pltpu
from jax.sharding import PartitionSpec as P

H = 64
KVH = 8
HD = 128
GQ = H // KVH
REACH = 7
SLAB = 2
BOTH = 2
FILL = -1e30


def halves_kernel(meta_ref, a_ref, b_ref, mine_ref, theirs_ref):
    mine_ref[...] = a_ref[...]
    theirs_ref[...] = b_ref[...]


def halves(kv, side):
    rows, half = kv.shape[0], kv.shape[1] // 4
    shape = (rows, half)
    return pl.pallas_call(
        halves_kernel,
        grid_spec=pltpu.PrefetchScalarGridSpec(
            num_scalar_prefetch=1,
            grid=(2,),
            in_specs=[
                pl.BlockSpec(shape, lambda i, m: (0, 2 * i + m[0])),
                pl.BlockSpec(shape, lambda i, m: (0, 2 * i + 1 - m[0])),
            ],
            out_specs=[pl.BlockSpec(shape, lambda i, m: (0, i))] * 2,
        ),
        out_shape=[jax.ShapeDtypeStruct((rows, 2 * half), kv.dtype)] * 2,
    )(side.reshape(1), kv, kv)


def attend_kernel(pairs, parts, tile, tiles, fresh, meta_ref, *refs):
    s_ref, top_ref = refs[-2:]
    inputs = 2 * parts + 4 * pairs
    if fresh:
        seg_ref, *ints_refs = refs[: 1 + parts]
        q_ref, *inputs = refs[1 + parts : 2 + parts + inputs]
        o_ref, bias_ref, reach_ref = refs[-5:-2]
    else:
        bias_ref, reach_ref, q_ref, *inputs = refs[: 3 + inputs]
        o_ref = refs[-3]
    pk_refs, pv_refs = inputs[:parts], inputs[parts : 2 * parts]
    k_refs, v_refs = inputs[2 * parts :][: 2 * pairs], inputs[2 * parts + 2 * pairs :]
    rows = q_ref.shape[0]
    step = 2 * rows
    span = pk_refs[0].shape[0]
    prefix_keys = parts * span
    block, limit = meta_ref[0], meta_ref[2]
    scale = math.log2(math.e) / math.sqrt(HD)
    nt = (((1,), (1,)), ((), ()))

    def masks():
        ints = jnp.concatenate([ref[...].astype(jnp.float32) for ref in ints_refs])
        row = lax.broadcasted_iota(jnp.int32, ints.shape, 0)
        part = lax.rem(row, tile)
        place = jnp.where(part == 0, pltpu.roll(ints, prefix_keys - 1, 0), ints)
        live = place.astype(jnp.int32) * tile + part < limit
        bias_ref[:, :prefix_keys] = jnp.where(live, 0.0, FILL).T

        own = seg_ref[...].astype(jnp.float32)
        has_segs = lax.rem(row, tiles * tile) == 0
        earlier = jnp.sum(jnp.where(has_segs & (ints < own[:, :1]), 1.0, 0.0))
        reach_ref[0] = lax.div(block, 2) - lax.div(earlier.astype(jnp.int32), step)

        seg_q = jnp.broadcast_to(own, (rows, rows)).T
        row_pos = block * rows + lax.broadcasted_iota(jnp.int32, (rows, rows), 0)
        lane = lax.broadcasted_iota(jnp.int32, (rows, rows), 1)
        for k in range(pairs):
            for j, first in enumerate((block, block + 1 - 2 * lax.rem(block, 2))):
                at = (2 * k + j) * tiles * tile
                seen = (ints[at : at + 1] == seg_q) & ((first - 2 * k) * rows + lane <= row_pos)
                at = prefix_keys + (2 * k + j) * rows
                bias_ref[:, at : at + rows] = jnp.where(seen, 0.0, FILL)

    if fresh:
        pl.when(pl.program_id(0) == 0)(masks)

    def body(near):
        each = step // span
        steps = prefix_keys // step + near + 1

        def score(slab):
            head = pl.ds(slab // (GQ // SLAB) * HD, HD)
            of = range(slab * SLAB, (slab + 1) * SLAB)
            q = jnp.concatenate([q_ref[:, g * HD : (g + 1) * HD] for g in of])
            refs_of = [pk_refs[at : at + each] for at in range(0, parts, each)]
            refs_of += [k_refs[2 * k : 2 * k + 2] for k in range(near + 1)]
            top = None
            for i in range(steps):
                at = slice(i * step, (i + 1) * step)
                keys = jnp.concatenate([ref[:, head] for ref in refs_of[i]])
                s = lax.dot_general(q, keys, nt, preferred_element_type=jnp.float32)
                s = (s.reshape(SLAB, rows, step) + bias_ref[:, at][None]).reshape(-1, step)
                s_ref[slab % 2, :, at] = s
                high = jnp.maximum(s[:, :rows], s[:, rows:])
                top = high if top is None else jnp.maximum(top, high)
            top = jnp.max(top, axis=1, keepdims=True)
            top_ref[slab % 2] = jnp.broadcast_to(top, (SLAB * rows, HD))

        def weigh(slab):
            head = pl.ds(slab // (GQ // SLAB) * HD, HD)
            values = [ref[:, head] for ref in (*pv_refs, *v_refs[: 2 * near + 2])]
            values = jnp.concatenate(values)
            values = jnp.concatenate([values, jnp.ones_like(values)], axis=1)
            top = top_ref[slab % 2]
            weights = [
                jnp.exp2((s_ref[slab % 2, :, i * HD : (i + 1) * HD] - top) * scale).astype(
                    jnp.bfloat16
                )
                for i in range(steps * step // HD)
            ]
            acc = jnp.dot(
                jnp.concatenate(weights, axis=1), values, preferred_element_type=jnp.float32
            )
            out = (acc[:, :HD] / acc[:, HD:]).astype(o_ref.dtype)
            for j in range(SLAB):
                g = slab * SLAB + j
                o_ref[:, g * HD : (g + 1) * HD] = out[j * rows : (j + 1) * rows]

        slabs = BOTH * GQ // SLAB
        score(0)
        for slab in range(slabs):
            if slab + 1 < slabs:
                score(slab + 1)
            weigh(slab)

    for near in range(pairs):
        pl.when(reach_ref[0] == near)(functools.partial(body, near))


def attend(meta, queries, pieces, prefix, tile, tiles, segments=None, before=None):
    rows = queries.shape[0]
    span = prefix[0].shape[0]
    pairs, parts = len(pieces) // 2, len(prefix)
    pieces, places = zip(*[piece if isinstance(piece, tuple) else (piece, 0) for piece in pieces])
    heads = pieces[0].shape[1] // (2 * HD)
    blocks = heads // BOTH
    keys = rows * len(pieces) + span * parts
    whole = pl.BlockSpec((rows, keys), lambda i, m: (0, 0))
    scalar = pl.BlockSpec(memory_space=pltpu.SMEM)
    wide = pl.BlockSpec((rows, BOTH * GQ * HD), lambda i, m: (0, m[1] + i))
    fresh = before is None
    queries, *arrays = [
        pltpu.with_memory_space_constraint(array, pltpu.HBM)
        for array in (queries, *prefix, *pieces)
    ]
    prefix, pieces = arrays[:parts], arrays[parts:]
    args = [meta, *([segments, *prefix] if fresh else before[1:])]
    args += [queries, *prefix, *prefix, *pieces, *pieces]
    if fresh:
        ints = pl.BlockSpec((span, rows), lambda i, m: (0, 2 * KVH))
        in_specs = [pl.BlockSpec((1, rows), lambda i, m: (0, 0)), *[ints] * parts]
    else:
        in_specs = [whole, scalar]
    in_specs += [
        wide,
        *[pl.BlockSpec((span, BOTH * HD), lambda i, m: (0, m[1] + i))] * parts,
        *[pl.BlockSpec((span, BOTH * HD), lambda i, m: (0, KVH // BOTH + m[1] + i))] * parts,
        *[pl.BlockSpec((rows, BOTH * HD), lambda i, m, at=at: (at, i)) for at in places],
        *[pl.BlockSpec((rows, BOTH * HD), lambda i, m, at=at: (at, blocks + i)) for at in places],
    ]
    out_specs = [wide]
    out_shape = [jax.ShapeDtypeStruct(queries.shape, queries.dtype)]
    aliases = {}
    if fresh:
        out_specs += [whole, scalar]
        out_shape += [
            jax.ShapeDtypeStruct((rows, keys), jnp.float32),
            jax.ShapeDtypeStruct((1,), jnp.int32),
        ]
    else:
        args.append(before[0])
        in_specs.append(pl.BlockSpec(memory_space=pl.ANY))
        aliases = {len(args) - 1: 0}
    return pl.pallas_call(
        functools.partial(attend_kernel, pairs, parts, tile, tiles, fresh),
        grid_spec=pltpu.PrefetchScalarGridSpec(
            num_scalar_prefetch=1,
            grid=(blocks,),
            in_specs=in_specs,
            out_specs=out_specs,
            scratch_shapes=[
                pltpu.VMEM((2, SLAB * rows, keys), jnp.float32),
                pltpu.VMEM((2, SLAB * rows, HD), jnp.float32),
            ],
        ),
        out_shape=out_shape,
        input_output_aliases=aliases,
        compiler_params=pltpu.CompilerParams(vmem_limit_bytes=24 * 1024 * 1024),
    )(*args)


def on_device(queries, resp_kv, resp_segments, prefix_kv, tile_plan, prompt_lengths):
    rows = queries.shape[1]
    tiles, tile, columns = prefix_kv.shape
    groups, count = lax.axis_size("prompt"), lax.axis_size("resp")
    group = lax.axis_index("prompt")
    block = lax.axis_index("resp")
    side = block % 2
    steps = min(count // 2 - 1, (REACH + 1) // 2)
    assert tiles == groups

    def swap(value, first):
        return lax.ppermute(value, "resp", [(r, r ^ 1) for r in range(2 * first, count)])

    def climb(value, step):
        pairs = [(r, r + 2) for r in range(2 * step - 2, count - 2)]
        return lax.ppermute(value, "resp", pairs)

    def shift(value, axis, by):
        size = lax.axis_size(axis)
        return lax.ppermute(value, axis, [(r, (r + by) % size) for r in range(size)])

    def after(value, *others):
        return lax.optimization_barrier((value, *others))[0]

    mine, theirs = halves(resp_kv[0], side)
    partner = swap(theirs, 0)
    upper = [(r, r + 1) for r in range(0, count, 2)]
    upper = lax.ppermute(after(mine, partner), "resp", upper)
    straight, crossed = [mine, partner], [theirs, upper]
    for step in range(1, steps + 1):
        one, two = straight[-2:]
        if step > 2:
            two = after(two, crossed[2][0], upper)
        one, two = climb(one, step), climb(two, step)
        straight += [one, two]
        if step < steps:
            both = swap(jnp.concatenate([two, one]), step)
            crossed += [(both, 0), (both, 1)]
        else:
            crossed += [swap(two, step), swap(one, step)]

    owners = (group + jnp.arange(groups, dtype=jnp.int32)) % groups
    pick = tile_plan[None, :, 0] == owners[:, None]
    place = jnp.sum(jnp.where(pick, tile_plan[None, :, 1], 0), axis=1, dtype=jnp.int32)
    own_tiles = jnp.sum(
        jnp.where(pick[:, :, None, None], prefix_kv[None], 0).astype(jnp.float32), axis=1
    )
    row = jnp.arange(tile, dtype=jnp.int32)[:, None]
    extra = jnp.where(row == 0, resp_segments[0], place.reshape(groups, 1, 1))
    own_tiles = jnp.concatenate([own_tiles, extra.astype(jnp.float32)], axis=-1)
    own_tiles = own_tiles.astype(prefix_kv.dtype)
    came = [own_tiles[0]] + [shift(own_tiles[by], "prompt", by) for by in range(1, groups)]
    came = jnp.concatenate(came)
    prefix = [jnp.concatenate([came, swap(came, 0)])]
    for by in range(1, count // 2):
        source = after(prefix[0], straight[min(2 * by + 1, len(straight) - 2)])
        prefix.append(shift(source, "resp", 2 * by))

    def meta(first):
        return jnp.stack([block, first * (KVH // 2 // BOTH), prompt_lengths[0]])

    done = attend(
        meta(side), queries[0], straight, prefix, tile, tiles, segments=resp_segments
    )
    done = attend(meta(1 - side), queries[0], crossed, prefix, tile, tiles, before=done)
    return done[0][None]


def solution(mesh):
    return jax.shard_map(
        on_device,
        mesh=mesh,
        in_specs=(
            P("prompt", "resp", None),
            P("prompt", "resp", None),
            P("prompt", "resp"),
            P(("prompt", "resp"), None, None),
            P(("prompt", "resp"), None),
            P("prompt"),
        ),
        out_specs=P("prompt", "resp", None),
        check_vma=False,
    )
```

```python
import functools
import math

import jax
import jax.numpy as jnp
from jax import lax
from jax.experimental import pallas as pl
from jax.experimental.pallas import tpu as pltpu
from jax.sharding import PartitionSpec as P

H = 64
KVH = 8
HD = 128
GQ = H // KVH
REACH = 7
SLAB = 2
BOTH = 2
FILL = -1e30


def halves_kernel(meta_ref, a_ref, b_ref, mine_ref, theirs_ref):
    mine_ref[...] = a_ref[...]
    theirs_ref[...] = b_ref[...]


def halves(kv, side):
    rows, half = kv.shape[0], kv.shape[1] // 4
    shape = (rows, half)
    return pl.pallas_call(
        halves_kernel,
        grid_spec=pltpu.PrefetchScalarGridSpec(
            num_scalar_prefetch=1,
            grid=(2,),
            in_specs=[
                pl.BlockSpec(shape, lambda i, m: (0, 2 * i + m[0])),
                pl.BlockSpec(shape, lambda i, m: (0, 2 * i + 1 - m[0])),
            ],
            out_specs=[pl.BlockSpec(shape, lambda i, m: (0, i))] * 2,
        ),
        out_shape=[jax.ShapeDtypeStruct((rows, 2 * half), kv.dtype)] * 2,
    )(side.reshape(1), kv, kv)


def attend_kernel(pairs, parts, tile, tiles, fresh, meta_ref, *refs):
    s_ref, top_ref = refs[-2:]
    inputs = 2 * parts + 4 * pairs
    if fresh:
        seg_ref, *ints_refs = refs[: 1 + parts]
        q_ref, *inputs = refs[1 + parts : 2 + parts + inputs]
        o_ref, bias_ref, reach_ref = refs[-5:-2]
    else:
        bias_ref, reach_ref, q_ref, *inputs = refs[: 3 + inputs]
        o_ref = refs[-3]
    pk_refs, pv_refs = inputs[:parts], inputs[parts : 2 * parts]
    k_refs, v_refs = inputs[2 * parts :][: 2 * pairs], inputs[2 * parts + 2 * pairs :]
    rows = q_ref.shape[0]
    step = 2 * rows
    span = pk_refs[0].shape[0]
    prefix_keys = parts * span
    block, limit = meta_ref[0], meta_ref[2]
    scale = math.log2(math.e) / math.sqrt(HD)
    nt = (((1,), (1,)), ((), ()))

    def masks():
        ints = jnp.concatenate([ref[...].astype(jnp.float32) for ref in ints_refs])
        row = lax.broadcasted_iota(jnp.int32, ints.shape, 0)
        part = lax.rem(row, tile)
        place = jnp.where(part == 0, pltpu.roll(ints, prefix_keys - 1, 0), ints)
        live = place.astype(jnp.int32) * tile + part < limit
        bias_ref[:, :prefix_keys] = jnp.where(live, 0.0, FILL).T

        own = seg_ref[...].astype(jnp.float32)
        has_segs = lax.rem(row, tiles * tile) == 0
        earlier = jnp.sum(jnp.where(has_segs & (ints < own[:, :1]), 1.0, 0.0))
        reach_ref[0] = lax.div(block, 2) - lax.div(earlier.astype(jnp.int32), step)

        seg_q = jnp.broadcast_to(own, (rows, rows)).T
        row_pos = block * rows + lax.broadcasted_iota(jnp.int32, (rows, rows), 0)
        lane = lax.broadcasted_iota(jnp.int32, (rows, rows), 1)
        for k in range(pairs):
            for j, first in enumerate((block, block + 1 - 2 * lax.rem(block, 2))):
                at = (2 * k + j) * tiles * tile
                seen = (ints[at : at + 1] == seg_q) & ((first - 2 * k) * rows + lane <= row_pos)
                at = prefix_keys + (2 * k + j) * rows
                bias_ref[:, at : at + rows] = jnp.where(seen, 0.0, FILL)

    if fresh:
        pl.when(pl.program_id(0) == 0)(masks)

    def body(near):
        each = step // span
        steps = prefix_keys // step + near + 1

        def score(slab):
            head = pl.ds(slab // (GQ // SLAB) * HD, HD)
            of = range(slab * SLAB, (slab + 1) * SLAB)
            q = jnp.concatenate([q_ref[:, g * HD : (g + 1) * HD] for g in of])
            refs_of = [pk_refs[at : at + each] for at in range(0, parts, each)]
            refs_of += [k_refs[2 * k : 2 * k + 2] for k in range(near + 1)]
            top = None
            for i in range(steps):
                at = slice(i * step, (i + 1) * step)
                keys = jnp.concatenate([ref[:, head] for ref in refs_of[i]])
                s = lax.dot_general(q, keys, nt, preferred_element_type=jnp.float32)
                s = (s.reshape(SLAB, rows, step) + bias_ref[:, at][None]).reshape(-1, step)
                s_ref[slab % 2, :, at] = s
                high = jnp.maximum(s[:, :rows], s[:, rows:])
                top = high if top is None else jnp.maximum(top, high)
            top = jnp.max(top, axis=1, keepdims=True)
            top_ref[slab % 2] = jnp.broadcast_to(top, (SLAB * rows, HD))

        def weigh(slab):
            head = pl.ds(slab // (GQ // SLAB) * HD, HD)
            values = [ref[:, head] for ref in (*pv_refs, *v_refs[: 2 * near + 2])]
            values = jnp.concatenate(values)
            values = jnp.concatenate([values, jnp.ones_like(values)], axis=1)
            top = top_ref[slab % 2]
            weights = [
                jnp.exp2((s_ref[slab % 2, :, i * HD : (i + 1) * HD] - top) * scale).astype(
                    jnp.bfloat16
                )
                for i in range(steps * step // HD)
            ]
            acc = jnp.dot(
                jnp.concatenate(weights, axis=1), values, preferred_element_type=jnp.float32
            )
            out = (acc[:, :HD] / acc[:, HD:]).astype(o_ref.dtype)
            for j in range(SLAB):
                g = slab * SLAB + j
                o_ref[:, g * HD : (g + 1) * HD] = out[j * rows : (j + 1) * rows]

        slabs = BOTH * GQ // SLAB
        score(0)
        for slab in range(slabs):
            if slab + 1 < slabs:
                score(slab + 1)
            weigh(slab)

    for near in range(pairs):
        pl.when(reach_ref[0] == near)(functools.partial(body, near))


def attend(meta, queries, pieces, prefix, tile, tiles, segments=None, before=None):
    rows = queries.shape[0]
    span = prefix[0].shape[0]
    pairs, parts = len(pieces) // 2, len(prefix)
    pieces, places = zip(*[piece if isinstance(piece, tuple) else (piece, 0) for piece in pieces])
    heads = pieces[0].shape[1] // (2 * HD)
    blocks = heads // BOTH
    keys = rows * len(pieces) + span * parts
    whole = pl.BlockSpec((rows, keys), lambda i, m: (0, 0))
    scalar = pl.BlockSpec(memory_space=pltpu.SMEM)
    wide = pl.BlockSpec((rows, BOTH * GQ * HD), lambda i, m: (0, m[1] + i))
    fresh = before is None
    queries, *arrays = [
        pltpu.with_memory_space_constraint(array, pltpu.HBM)
        for array in (queries, *prefix, *pieces)
    ]
    prefix, pieces = arrays[:parts], arrays[parts:]
    args = [meta, *([segments, *prefix] if fresh else before[1:])]
    args += [queries, *prefix, *prefix, *pieces, *pieces]
    if fresh:
        ints = pl.BlockSpec((span, rows), lambda i, m: (0, 2 * KVH))
        in_specs = [pl.BlockSpec((1, rows), lambda i, m: (0, 0)), *[ints] * parts]
    else:
        in_specs = [whole, scalar]
    in_specs += [
        wide,
        *[pl.BlockSpec((span, BOTH * HD), lambda i, m: (0, m[1] + i))] * parts,
        *[pl.BlockSpec((span, BOTH * HD), lambda i, m: (0, KVH // BOTH + m[1] + i))] * parts,
        *[pl.BlockSpec((rows, BOTH * HD), lambda i, m, at=at: (at, i)) for at in places],
        *[pl.BlockSpec((rows, BOTH * HD), lambda i, m, at=at: (at, blocks + i)) for at in places],
    ]
    out_specs = [wide]
    out_shape = [jax.ShapeDtypeStruct(queries.shape, queries.dtype)]
    aliases = {}
    if fresh:
        out_specs += [whole, scalar]
        out_shape += [
            jax.ShapeDtypeStruct((rows, keys), jnp.float32),
            jax.ShapeDtypeStruct((1,), jnp.int32),
        ]
    else:
        args.append(before[0])
        in_specs.append(pl.BlockSpec(memory_space=pl.ANY))
        aliases = {len(args) - 1: 0}
    return pl.pallas_call(
        functools.partial(attend_kernel, pairs, parts, tile, tiles, fresh),
        grid_spec=pltpu.PrefetchScalarGridSpec(
            num_scalar_prefetch=1,
            grid=(blocks,),
            in_specs=in_specs,
            out_specs=out_specs,
            scratch_shapes=[
                pltpu.VMEM((2, SLAB * rows, keys), jnp.float32),
                pltpu.VMEM((2, SLAB * rows, HD), jnp.float32),
            ],
        ),
        out_shape=out_shape,
        input_output_aliases=aliases,
        compiler_params=pltpu.CompilerParams(vmem_limit_bytes=24 * 1024 * 1024),
    )(*args)


def on_device(queries, resp_kv, resp_segments, prefix_kv, tile_plan, prompt_lengths):
    rows = queries.shape[1]
    tiles, tile, columns = prefix_kv.shape
    groups, count = lax.axis_size("prompt"), lax.axis_size("resp")
    group = lax.axis_index("prompt")
    block = lax.axis_index("resp")
    side = block % 2
    steps = min(count // 2 - 1, (REACH + 1) // 2)
    assert tiles == groups

    def swap(value, first):
        return lax.ppermute(value, "resp", [(r, r ^ 1) for r in range(2 * first, count)])

    def climb(value, step):
        pairs = [(r, r + 2) for r in range(2 * step - 2, count - 2)]
        return lax.ppermute(value, "resp", pairs)

    def shift(value, axis, by):
        size = lax.axis_size(axis)
        return lax.ppermute(value, axis, [(r, (r + by) % size) for r in range(size)])

    def after(value, *others):
        return lax.optimization_barrier((value, *others))[0]

    mine, theirs = halves(resp_kv[0], side)
    partner = swap(theirs, 0)
    upper = [(r, r + 1) for r in range(0, count, 2)]
    upper = lax.ppermute(after(mine, partner), "resp", upper)
    straight, crossed = [mine, partner], [theirs, upper]
    for step in range(1, steps + 1):
        one, two = straight[-2:]
        if step > 2:
            one, two = after(one, crossed[-3]), after(two, crossed[-4], upper)
        one, two = climb(one, step), climb(two, step)
        straight += [one, two]
        crossed += [swap(two, step), swap(one, step)]

    owners = (group + jnp.arange(groups, dtype=jnp.int32)) % groups
    pick = tile_plan[None, :, 0] == owners[:, None]
    place = jnp.sum(jnp.where(pick, tile_plan[None, :, 1], 0), axis=1, dtype=jnp.int32)
    own_tiles = jnp.sum(
        jnp.where(pick[:, :, None, None], prefix_kv[None], 0).astype(jnp.float32), axis=1
    )
    row = jnp.arange(tile, dtype=jnp.int32)[:, None]
    extra = jnp.where(row == 0, resp_segments[0], place.reshape(groups, 1, 1))
    own_tiles = jnp.concatenate([own_tiles, extra.astype(jnp.float32)], axis=-1)
    own_tiles = own_tiles.astype(prefix_kv.dtype)
    came = [own_tiles[0]] + [shift(own_tiles[by], "prompt", by) for by in range(1, groups)]
    came = jnp.concatenate(came)
    prefix = [jnp.concatenate([came, swap(came, 0)])]
    behind = [(), (crossed[5], straight[5]), (straight[6],)]
    for by in range(1, count // 2):
        source = after(prefix[0], *behind[min(by, len(behind)) - 1])
        prefix.append(shift(source, "resp", 2 * by))

    def meta(first):
        return jnp.stack([block, first * (KVH // 2 // BOTH), prompt_lengths[0]])

    done = attend(
        meta(side), queries[0], straight, prefix, tile, tiles, segments=resp_segments
    )
    done = attend(meta(1 - side), queries[0], crossed, prefix, tile, tiles, before=done)
    return done[0][None]


def solution(mesh):
    return jax.shard_map(
        on_device,
        mesh=mesh,
        in_specs=(
            P("prompt", "resp", None),
            P("prompt", "resp", None),
            P("prompt", "resp"),
            P(("prompt", "resp"), None, None),
            P(("prompt", "resp"), None),
            P("prompt"),
        ),
        out_specs=P("prompt", "resp", None),
        check_vma=False,
    )
```

```python
import functools
import math

import jax
import jax.numpy as jnp
from jax import lax
from jax.experimental import pallas as pl
from jax.experimental.pallas import tpu as pltpu
from jax.sharding import PartitionSpec as P

H = 64
KVH = 8
HD = 128
GQ = H // KVH
REACH = 7
SLAB = 2
BOTH = 2
FILL = -1e30


def halves_kernel(meta_ref, a_ref, b_ref, mine_ref, theirs_ref):
    mine_ref[...] = a_ref[...]
    theirs_ref[...] = b_ref[...]


def halves(kv, side):
    rows, half = kv.shape[0], kv.shape[1] // 4
    shape = (rows, half)
    return pl.pallas_call(
        halves_kernel,
        grid_spec=pltpu.PrefetchScalarGridSpec(
            num_scalar_prefetch=1,
            grid=(2,),
            in_specs=[
                pl.BlockSpec(shape, lambda i, m: (0, 2 * i + m[0])),
                pl.BlockSpec(shape, lambda i, m: (0, 2 * i + 1 - m[0])),
            ],
            out_specs=[pl.BlockSpec(shape, lambda i, m: (0, i))] * 2,
        ),
        out_shape=[jax.ShapeDtypeStruct((rows, 2 * half), kv.dtype)] * 2,
    )(side.reshape(1), kv, kv)


def attend_kernel(pairs, parts, tile, tiles, meta_ref, seg_ref, *refs):
    o_ref, bias_ref, reach_ref, s_ref, top_ref = refs[-5:]
    ints_refs, (q_ref, *refs) = refs[:parts], refs[parts:-5]
    pk_refs, pv_refs, refs = refs[:parts], refs[parts : 2 * parts], refs[2 * parts :]
    halves_refs = [
        (refs[at : at + 2 * pairs], refs[at + 2 * pairs : at + 4 * pairs])
        for at in (0, 4 * pairs)
    ]
    rows = q_ref.shape[0]
    step = 2 * rows
    span = pk_refs[0].shape[0]
    prefix_keys = parts * span
    block, limit = meta_ref[0], meta_ref[3]
    scale = math.log2(math.e) / math.sqrt(HD)
    nt = (((1,), (1,)), ((), ()))

    def masks():
        ints = jnp.concatenate([ref[...].astype(jnp.float32) for ref in ints_refs])
        row = lax.broadcasted_iota(jnp.int32, ints.shape, 0)
        part = lax.rem(row, tile)
        place = jnp.where(part == 0, pltpu.roll(ints, prefix_keys - 1, 0), ints)
        live = place.astype(jnp.int32) * tile + part < limit
        bias_ref[:, :prefix_keys] = jnp.where(live, 0.0, FILL).T

        own = seg_ref[...].astype(jnp.float32)
        has_segs = lax.rem(row, tiles * tile) == 0
        earlier = jnp.sum(jnp.where(has_segs & (ints < own[:, :1]), 1.0, 0.0))
        reach_ref[0] = lax.div(block, 2) - lax.div(earlier.astype(jnp.int32), step)

        seg_q = jnp.broadcast_to(own, (rows, rows)).T
        row_pos = block * rows + lax.broadcasted_iota(jnp.int32, (rows, rows), 0)
        lane = lax.broadcasted_iota(jnp.int32, (rows, rows), 1)
        for k in range(pairs):
            for j, first in enumerate((block, block + 1 - 2 * lax.rem(block, 2))):
                at = (2 * k + j) * tiles * tile
                seen = (ints[at : at + 1] == seg_q) & ((first - 2 * k) * rows + lane <= row_pos)
                at = prefix_keys + (2 * k + j) * rows
                bias_ref[:, at : at + rows] = jnp.where(seen, 0.0, FILL)

    pl.when(pl.program_id(0) == 0)(masks)

    def body(near, k_refs, v_refs):
        each = step // span
        steps = prefix_keys // step + near + 1

        def score(slab):
            head = pl.ds(slab // (GQ // SLAB) * HD, HD)
            of = range(slab * SLAB, (slab + 1) * SLAB)
            q = jnp.concatenate([q_ref[:, g * HD : (g + 1) * HD] for g in of])
            refs_of = [pk_refs[at : at + each] for at in range(0, parts, each)]
            refs_of += [k_refs[2 * k : 2 * k + 2] for k in range(near + 1)]
            top = None
            for i in range(steps):
                at = slice(i * step, (i + 1) * step)
                keys = jnp.concatenate([ref[:, head] for ref in refs_of[i]])
                s = lax.dot_general(q, keys, nt, preferred_element_type=jnp.float32)
                s = (s.reshape(SLAB, rows, step) + bias_ref[:, at][None]).reshape(-1, step)
                s_ref[slab % 2, :, at] = s
                high = jnp.maximum(s[:, :rows], s[:, rows:])
                top = high if top is None else jnp.maximum(top, high)
            top = jnp.max(top, axis=1, keepdims=True)
            top_ref[slab % 2] = jnp.broadcast_to(top, (SLAB * rows, HD))

        def weigh(slab):
            head = pl.ds(slab // (GQ // SLAB) * HD, HD)
            values = [ref[:, head] for ref in (*pv_refs, *v_refs[: 2 * near + 2])]
            values = jnp.concatenate(values)
            values = jnp.concatenate([values, jnp.ones_like(values)], axis=1)
            top = top_ref[slab % 2]
            weights = [
                jnp.exp2((s_ref[slab % 2, :, i * HD : (i + 1) * HD] - top) * scale).astype(
                    jnp.bfloat16
                )
                for i in range(steps * step // HD)
            ]
            acc = jnp.dot(
                jnp.concatenate(weights, axis=1), values, preferred_element_type=jnp.float32
            )
            out = (acc[:, :HD] / acc[:, HD:]).astype(o_ref.dtype)
            for j in range(SLAB):
                g = slab * SLAB + j
                o_ref[:, g * HD : (g + 1) * HD] = out[j * rows : (j + 1) * rows]

        slabs = BOTH * GQ // SLAB
        score(0)
        for slab in range(slabs):
            if slab + 1 < slabs:
                score(slab + 1)
            weigh(slab)

    second = pl.program_id(0) >= pl.num_programs(0) // 2
    for half, refs_of_half in enumerate(halves_refs):
        for near in range(pairs):
            due = (reach_ref[0] == near) & (second == bool(half))
            pl.when(due)(functools.partial(body, near, *refs_of_half))


def attend(meta, segments, queries, straight, crossed, prefix, tile, tiles):
    rows = queries.shape[0]
    span = prefix[0].shape[0]
    pairs, parts = len(straight) // 2, len(prefix)
    blocks = straight[0].shape[1] // (2 * HD) // BOTH
    keys = rows * len(straight) + span * parts

    def head(i, m):
        return jnp.where(i < blocks, m[1] + i, m[2] + i - blocks)

    def own(i):
        return jnp.minimum(i, blocks - 1)

    def other(i):
        return jnp.maximum(i - blocks, 0)

    wide = pl.BlockSpec((rows, BOTH * GQ * HD), lambda i, m: (0, head(i, m)))
    shape = (rows, BOTH * HD)
    queries, *arrays = [
        pltpu.with_memory_space_constraint(array, pltpu.HBM)
        for array in (queries, *prefix, *straight, *crossed)
    ]
    prefix, straight, crossed = (
        arrays[:parts],
        arrays[parts : parts + 2 * pairs],
        arrays[parts + 2 * pairs :],
    )
    values_at = KVH // BOTH
    in_specs = [
        pl.BlockSpec((1, rows), lambda i, m: (0, 0)),
        *[pl.BlockSpec((span, rows), lambda i, m: (0, 2 * KVH))] * parts,
        wide,
        *[pl.BlockSpec((span, BOTH * HD), lambda i, m: (0, head(i, m)))] * parts,
        *[pl.BlockSpec((span, BOTH * HD), lambda i, m: (0, values_at + head(i, m)))] * parts,
        *[pl.BlockSpec(shape, lambda i, m: (0, own(i)))] * (2 * pairs),
        *[pl.BlockSpec(shape, lambda i, m: (0, blocks + own(i)))] * (2 * pairs),
        *[pl.BlockSpec(shape, lambda i, m: (0, other(i)))] * (2 * pairs),
        *[pl.BlockSpec(shape, lambda i, m: (0, blocks + other(i)))] * (2 * pairs),
    ]
    args = [segments, *prefix, queries, *prefix, *prefix]
    args += [*straight, *straight, *crossed, *crossed]
    return pl.pallas_call(
        functools.partial(attend_kernel, pairs, parts, tile, tiles),
        grid_spec=pltpu.PrefetchScalarGridSpec(
            num_scalar_prefetch=1,
            grid=(2 * blocks,),
            in_specs=in_specs,
            out_specs=wide,
            scratch_shapes=[
                pltpu.VMEM((rows, keys), jnp.float32),
                pltpu.SMEM((1,), jnp.int32),
                pltpu.VMEM((2, SLAB * rows, keys), jnp.float32),
                pltpu.VMEM((2, SLAB * rows, HD), jnp.float32),
            ],
        ),
        out_shape=jax.ShapeDtypeStruct(queries.shape, queries.dtype),
        compiler_params=pltpu.CompilerParams(vmem_limit_bytes=32 * 1024 * 1024),
    )(meta, *args)


def on_device(queries, resp_kv, resp_segments, prefix_kv, tile_plan, prompt_lengths):
    rows = queries.shape[1]
    tiles, tile, columns = prefix_kv.shape
    groups, count = lax.axis_size("prompt"), lax.axis_size("resp")
    group = lax.axis_index("prompt")
    block = lax.axis_index("resp")
    side = block % 2
    steps = min(count // 2 - 1, (REACH + 1) // 2)
    assert tiles == groups

    def swap(value, first):
        return lax.ppermute(value, "resp", [(r, r ^ 1) for r in range(2 * first, count)])

    def climb(value, step):
        pairs = [(r, r + 2) for r in range(2 * step - 2, count - 2)]
        return lax.ppermute(value, "resp", pairs)

    def shift(value, axis, by):
        size = lax.axis_size(axis)
        return lax.ppermute(value, axis, [(r, (r + by) % size) for r in range(size)])

    def after(value, *others):
        return lax.optimization_barrier((value, *others))[0]

    mine, theirs = halves(resp_kv[0], side)
    partner = swap(theirs, 0)
    upper = [(r, r + 1) for r in range(0, count, 2)]
    upper = lax.ppermute(after(mine, partner), "resp", upper)
    straight, crossed = [mine, partner], [theirs, upper]
    for step in range(1, steps + 1):
        one, two = straight[-2:]
        if step > 2:
            one, two = after(one, crossed[-3]), after(two, crossed[-4], upper)
        one, two = climb(one, step), climb(two, step)
        straight += [one, two]
        crossed += [swap(two, step), swap(one, step)]

    owners = (group + jnp.arange(groups, dtype=jnp.int32)) % groups
    pick = tile_plan[None, :, 0] == owners[:, None]
    place = jnp.sum(jnp.where(pick, tile_plan[None, :, 1], 0), axis=1, dtype=jnp.int32)
    own_tiles = jnp.sum(
        jnp.where(pick[:, :, None, None], prefix_kv[None], 0).astype(jnp.float32), axis=1
    )
    row = jnp.arange(tile, dtype=jnp.int32)[:, None]
    extra = jnp.where(row == 0, resp_segments[0], place.reshape(groups, 1, 1))
    own_tiles = jnp.concatenate([own_tiles, extra.astype(jnp.float32)], axis=-1)
    own_tiles = own_tiles.astype(prefix_kv.dtype)
    came = [own_tiles[0]] + [shift(own_tiles[by], "prompt", by) for by in range(1, groups)]
    came = jnp.concatenate(came)
    prefix = [jnp.concatenate([came, swap(came, 0)])]
    behind = [(), (crossed[5], straight[5]), (straight[6],)]
    for by in range(1, count // 2):
        source = after(prefix[0], *behind[min(by, len(behind)) - 1])
        prefix.append(shift(source, "resp", 2 * by))

    first = KVH // 2 // BOTH
    meta = jnp.stack([block, side * first, (1 - side) * first, prompt_lengths[0]])
    out = attend(
        meta, resp_segments, queries[0], straight, crossed, prefix, tile, tiles
    )
    return out[None]


def solution(mesh):
    return jax.shard_map(
        on_device,
        mesh=mesh,
        in_specs=(
            P("prompt", "resp", None),
            P("prompt", "resp", None),
            P("prompt", "resp"),
            P(("prompt", "resp"), None, None),
            P(("prompt", "resp"), None),
            P("prompt"),
        ),
        out_specs=P("prompt", "resp", None),
        check_vma=False,
    )
```

```python
import functools
import math

import jax
import jax.numpy as jnp
from jax import lax
from jax.experimental import pallas as pl
from jax.experimental.pallas import tpu as pltpu
from jax.sharding import PartitionSpec as P

H = 64
KVH = 8
HD = 128
GQ = H // KVH
REACH = 7
SLAB = 4
BOTH = 2
FILL = -1e30


def halves_kernel(meta_ref, a_ref, b_ref, mine_ref, theirs_ref):
    mine_ref[...] = a_ref[...]
    theirs_ref[...] = b_ref[...]


def halves(kv, side):
    rows, half = kv.shape[0], kv.shape[1] // 4
    shape = (rows, half)
    return pl.pallas_call(
        halves_kernel,
        grid_spec=pltpu.PrefetchScalarGridSpec(
            num_scalar_prefetch=1,
            grid=(2,),
            in_specs=[
                pl.BlockSpec(shape, lambda i, m: (0, 2 * i + m[0])),
                pl.BlockSpec(shape, lambda i, m: (0, 2 * i + 1 - m[0])),
            ],
            out_specs=[pl.BlockSpec(shape, lambda i, m: (0, i))] * 2,
        ),
        out_shape=[jax.ShapeDtypeStruct((rows, 2 * half), kv.dtype)] * 2,
    )(side.reshape(1), kv, kv)


def attend_kernel(pairs, parts, tile, tiles, fresh, meta_ref, *refs):
    s_ref, top_ref = refs[-2:]
    inputs = 2 * parts + 4 * pairs
    if fresh:
        seg_ref, *ints_refs = refs[: 1 + parts]
        q_ref, *inputs = refs[1 + parts : 2 + parts + inputs]
        o_ref, bias_ref, reach_ref = refs[-5:-2]
    else:
        bias_ref, reach_ref, q_ref, *inputs = refs[: 3 + inputs]
        o_ref = refs[-3]
    pk_refs, pv_refs = inputs[:parts], inputs[parts : 2 * parts]
    k_refs, v_refs = inputs[2 * parts :][: 2 * pairs], inputs[2 * parts + 2 * pairs :]
    rows = q_ref.shape[0]
    step = 2 * rows
    span = pk_refs[0].shape[0]
    prefix_keys = parts * span
    block, limit = meta_ref[0], meta_ref[2]
    scale = math.log2(math.e) / math.sqrt(HD)
    nt = (((1,), (1,)), ((), ()))

    def masks():
        ints = jnp.concatenate([ref[...].astype(jnp.float32) for ref in ints_refs])
        row = lax.broadcasted_iota(jnp.int32, ints.shape, 0)
        part = lax.rem(row, tile)
        place = jnp.where(part == 0, pltpu.roll(ints, prefix_keys - 1, 0), ints)
        live = place.astype(jnp.int32) * tile + part < limit
        bias_ref[:, :prefix_keys] = jnp.where(live, 0.0, FILL).T

        own = seg_ref[...].astype(jnp.float32)
        has_segs = lax.rem(row, tiles * tile) == 0
        earlier = jnp.sum(jnp.where(has_segs & (ints < own[:, :1]), 1.0, 0.0))
        reach_ref[0] = lax.div(block, 2) - lax.div(earlier.astype(jnp.int32), step)

        seg_q = jnp.broadcast_to(own, (rows, rows)).T
        row_pos = block * rows + lax.broadcasted_iota(jnp.int32, (rows, rows), 0)
        lane = lax.broadcasted_iota(jnp.int32, (rows, rows), 1)
        for k in range(pairs):
            for j, first in enumerate((block, block + 1 - 2 * lax.rem(block, 2))):
                at = (2 * k + j) * tiles * tile
                seen = (ints[at : at + 1] == seg_q) & ((first - 2 * k) * rows + lane <= row_pos)
                at = prefix_keys + (2 * k + j) * rows
                bias_ref[:, at : at + rows] = jnp.where(seen, 0.0, FILL)

    if fresh:
        pl.when(pl.program_id(0) == 0)(masks)

    def body(near):
        each = step // span
        steps = prefix_keys // step + near + 1

        def score(slab):
            head = pl.ds(slab // (GQ // SLAB) * HD, HD)
            of = range(slab * SLAB, (slab + 1) * SLAB)
            q = jnp.concatenate([q_ref[:, g * HD : (g + 1) * HD] for g in of])
            refs_of = [pk_refs[at : at + each] for at in range(0, parts, each)]
            refs_of += [k_refs[2 * k : 2 * k + 2] for k in range(near + 1)]
            top = None
            for i in range(steps):
                at = slice(i * step, (i + 1) * step)
                keys = jnp.concatenate([ref[:, head] for ref in refs_of[i]])
                s = lax.dot_general(q, keys, nt, preferred_element_type=jnp.float32)
                s = (s.reshape(SLAB, rows, step) + bias_ref[:, at][None]).reshape(-1, step)
                s_ref[slab % 2, :, at] = s
                high = jnp.maximum(s[:, :rows], s[:, rows:])
                top = high if top is None else jnp.maximum(top, high)
            top = jnp.max(top, axis=1, keepdims=True)
            top_ref[slab % 2] = jnp.broadcast_to(top, (SLAB * rows, HD))

        def weigh(slab):
            head = pl.ds(slab // (GQ // SLAB) * HD, HD)
            values = [ref[:, head] for ref in (*pv_refs, *v_refs[: 2 * near + 2])]
            values = jnp.concatenate(values)
            values = jnp.concatenate([values, jnp.ones_like(values)], axis=1)
            top = top_ref[slab % 2]
            weights = [
                jnp.exp2((s_ref[slab % 2, :, i * HD : (i + 1) * HD] - top) * scale).astype(
                    jnp.bfloat16
                )
                for i in range(steps * step // HD)
            ]
            acc = jnp.dot(
                jnp.concatenate(weights, axis=1), values, preferred_element_type=jnp.float32
            )
            out = (acc[:, :HD] / acc[:, HD:]).astype(o_ref.dtype)
            for j in range(SLAB):
                g = slab * SLAB + j
                o_ref[:, g * HD : (g + 1) * HD] = out[j * rows : (j + 1) * rows]

        slabs = BOTH * GQ // SLAB
        score(0)
        for slab in range(slabs):
            if slab + 1 < slabs:
                score(slab + 1)
            weigh(slab)

    for near in range(pairs):
        pl.when(reach_ref[0] == near)(functools.partial(body, near))


def attend(meta, queries, pieces, prefix, tile, tiles, segments=None, before=None):
    rows = queries.shape[0]
    span = prefix[0].shape[0]
    pairs, parts = len(pieces) // 2, len(prefix)
    pieces, places = zip(*[piece if isinstance(piece, tuple) else (piece, 0) for piece in pieces])
    heads = pieces[0].shape[1] // (2 * HD)
    blocks = heads // BOTH
    keys = rows * len(pieces) + span * parts
    whole = pl.BlockSpec((rows, keys), lambda i, m: (0, 0))
    scalar = pl.BlockSpec(memory_space=pltpu.SMEM)
    wide = pl.BlockSpec((rows, BOTH * GQ * HD), lambda i, m: (0, m[1] + i))
    fresh = before is None
    queries, *arrays = [
        pltpu.with_memory_space_constraint(array, pltpu.HBM)
        for array in (queries, *prefix, *pieces)
    ]
    prefix, pieces = arrays[:parts], arrays[parts:]
    args = [meta, *([segments, *prefix] if fresh else before[1:])]
    args += [queries, *prefix, *prefix, *pieces, *pieces]
    if fresh:
        ints = pl.BlockSpec((span, rows), lambda i, m: (0, 2 * KVH))
        in_specs = [pl.BlockSpec((1, rows), lambda i, m: (0, 0)), *[ints] * parts]
    else:
        in_specs = [whole, scalar]
    in_specs += [
        wide,
        *[pl.BlockSpec((span, BOTH * HD), lambda i, m: (0, m[1] + i))] * parts,
        *[pl.BlockSpec((span, BOTH * HD), lambda i, m: (0, KVH // BOTH + m[1] + i))] * parts,
        *[pl.BlockSpec((rows, BOTH * HD), lambda i, m, at=at: (at, i)) for at in places],
        *[pl.BlockSpec((rows, BOTH * HD), lambda i, m, at=at: (at, blocks + i)) for at in places],
    ]
    out_specs = [wide]
    out_shape = [jax.ShapeDtypeStruct(queries.shape, queries.dtype)]
    aliases = {}
    if fresh:
        out_specs += [whole, scalar]
        out_shape += [
            jax.ShapeDtypeStruct((rows, keys), jnp.float32),
            jax.ShapeDtypeStruct((1,), jnp.int32),
        ]
    else:
        args.append(before[0])
        in_specs.append(pl.BlockSpec(memory_space=pl.ANY))
        aliases = {len(args) - 1: 0}
    return pl.pallas_call(
        functools.partial(attend_kernel, pairs, parts, tile, tiles, fresh),
        grid_spec=pltpu.PrefetchScalarGridSpec(
            num_scalar_prefetch=1,
            grid=(blocks,),
            in_specs=in_specs,
            out_specs=out_specs,
            scratch_shapes=[
                pltpu.VMEM((2, SLAB * rows, keys), jnp.float32),
                pltpu.VMEM((2, SLAB * rows, HD), jnp.float32),
            ],
        ),
        out_shape=out_shape,
        input_output_aliases=aliases,
        compiler_params=pltpu.CompilerParams(vmem_limit_bytes=32 * 1024 * 1024),
    )(*args)


def on_device(queries, resp_kv, resp_segments, prefix_kv, tile_plan, prompt_lengths):
    rows = queries.shape[1]
    tiles, tile, columns = prefix_kv.shape
    groups, count = lax.axis_size("prompt"), lax.axis_size("resp")
    group = lax.axis_index("prompt")
    block = lax.axis_index("resp")
    side = block % 2
    steps = min(count // 2 - 1, (REACH + 1) // 2)
    assert tiles == groups

    def swap(value, first):
        return lax.ppermute(value, "resp", [(r, r ^ 1) for r in range(2 * first, count)])

    def climb(value, step):
        pairs = [(r, r + 2) for r in range(2 * step - 2, count - 2)]
        return lax.ppermute(value, "resp", pairs)

    def shift(value, axis, by):
        size = lax.axis_size(axis)
        return lax.ppermute(value, axis, [(r, (r + by) % size) for r in range(size)])

    def after(value, *others):
        return lax.optimization_barrier((value, *others))[0]

    mine, theirs = halves(resp_kv[0], side)
    partner = swap(theirs, 0)
    upper = [(r, r + 1) for r in range(0, count, 2)]
    upper = lax.ppermute(after(mine, partner), "resp", upper)
    straight, crossed = [mine, partner], [theirs, upper]
    for step in range(1, steps + 1):
        one, two = straight[-2:]
        if step > 2:
            one, two = after(one, crossed[-3]), after(two, crossed[-4], upper)
        one, two = climb(one, step), climb(two, step)
        straight += [one, two]
        crossed += [swap(two, step), swap(one, step)]

    owners = (group + jnp.arange(groups, dtype=jnp.int32)) % groups
    pick = tile_plan[None, :, 0] == owners[:, None]
    place = jnp.sum(jnp.where(pick, tile_plan[None, :, 1], 0), axis=1, dtype=jnp.int32)
    own_tiles = jnp.sum(
        jnp.where(pick[:, :, None, None], prefix_kv[None], 0).astype(jnp.float32), axis=1
    )
    row = jnp.arange(tile, dtype=jnp.int32)[:, None]
    extra = jnp.where(row == 0, resp_segments[0], place.reshape(groups, 1, 1))
    own_tiles = jnp.concatenate([own_tiles, extra.astype(jnp.float32)], axis=-1)
    own_tiles = own_tiles.astype(prefix_kv.dtype)
    came = [own_tiles[0]] + [shift(own_tiles[by], "prompt", by) for by in range(1, groups)]
    came = jnp.concatenate(came)
    prefix = [jnp.concatenate([came, swap(came, 0)])]
    behind = [(), (crossed[5], straight[5]), (straight[6],)]
    for by in range(1, count // 2):
        source = after(prefix[0], *behind[min(by, len(behind)) - 1])
        prefix.append(shift(source, "resp", 2 * by))

    def meta(first):
        return jnp.stack([block, first * (KVH // 2 // BOTH), prompt_lengths[0]])

    done = attend(
        meta(side), queries[0], straight, prefix, tile, tiles, segments=resp_segments
    )
    done = attend(meta(1 - side), queries[0], crossed, prefix, tile, tiles, before=done)
    return done[0][None]


def solution(mesh):
    return jax.shard_map(
        on_device,
        mesh=mesh,
        in_specs=(
            P("prompt", "resp", None),
            P("prompt", "resp", None),
            P("prompt", "resp"),
            P(("prompt", "resp"), None, None),
            P(("prompt", "resp"), None),
            P("prompt"),
        ),
        out_specs=P("prompt", "resp", None),
        check_vma=False,
    )
```

```python
import functools
import math

import jax
import jax.numpy as jnp
from jax import lax
from jax.experimental import pallas as pl
from jax.experimental.pallas import tpu as pltpu
from jax.sharding import PartitionSpec as P

H = 64
KVH = 8
HD = 128
GQ = H // KVH
REACH = 7
SLAB = 4
BOTH = 2
FILL = -1e30


def halves_kernel(meta_ref, *refs):
    half = refs[0].shape[1]
    for i, ref in enumerate(refs[:4]):
        refs[4 + i // 2][:, i % 2 * half : (i % 2 + 1) * half] = ref[...]


def halves(kv, side):
    rows, half = kv.shape[0], kv.shape[1] // 4
    shape = (rows, half)
    return pl.pallas_call(
        halves_kernel,
        grid_spec=pltpu.PrefetchScalarGridSpec(
            num_scalar_prefetch=1,
            grid=(1,),
            in_specs=[
                pl.BlockSpec(shape, lambda i, m: (0, m[0])),
                pl.BlockSpec(shape, lambda i, m: (0, 2 + m[0])),
                pl.BlockSpec(shape, lambda i, m: (0, 1 - m[0])),
                pl.BlockSpec(shape, lambda i, m: (0, 3 - m[0])),
            ],
            out_specs=[pl.BlockSpec((rows, 2 * half), lambda i, m: (0, 0))] * 2,
        ),
        out_shape=[jax.ShapeDtypeStruct((rows, 2 * half), kv.dtype)] * 2,
    )(side.reshape(1), kv, kv, kv, kv)


def attend_kernel(pairs, parts, tile, tiles, fresh, meta_ref, *refs):
    s_ref, top_ref = refs[-2:]
    inputs = 2 * parts + 4 * pairs
    if fresh:
        seg_ref, *ints_refs = refs[: 1 + parts]
        q_ref, *inputs = refs[1 + parts : 2 + parts + inputs]
        o_ref, bias_ref, reach_ref = refs[-5:-2]
    else:
        bias_ref, reach_ref, q_ref, *inputs = refs[: 3 + inputs]
        o_ref = refs[-3]
    pk_refs, pv_refs = inputs[:parts], inputs[parts : 2 * parts]
    k_refs, v_refs = inputs[2 * parts :][: 2 * pairs], inputs[2 * parts + 2 * pairs :]
    rows = q_ref.shape[0]
    step = 2 * rows
    span = pk_refs[0].shape[0]
    prefix_keys = parts * span
    block, limit = meta_ref[0], meta_ref[2]
    scale = math.log2(math.e) / math.sqrt(HD)
    nt = (((1,), (1,)), ((), ()))

    def masks():
        ints = jnp.concatenate([ref[...].astype(jnp.float32) for ref in ints_refs])
        row = lax.broadcasted_iota(jnp.int32, ints.shape, 0)
        part = lax.rem(row, tile)
        place = jnp.where(part == 0, pltpu.roll(ints, prefix_keys - 1, 0), ints)
        live = place.astype(jnp.int32) * tile + part < limit
        bias_ref[:, :prefix_keys] = jnp.where(live, 0.0, FILL).T

        own = seg_ref[...].astype(jnp.float32)
        has_segs = lax.rem(row, tiles * tile) == 0
        earlier = jnp.sum(jnp.where(has_segs & (ints < own[:, :1]), 1.0, 0.0))
        reach_ref[0] = lax.div(block, 2) - lax.div(earlier.astype(jnp.int32), step)

        seg_q = jnp.broadcast_to(own, (rows, rows)).T
        row_pos = block * rows + lax.broadcasted_iota(jnp.int32, (rows, rows), 0)
        lane = lax.broadcasted_iota(jnp.int32, (rows, rows), 1)
        for k in range(pairs):
            for j, first in enumerate((block, block + 1 - 2 * lax.rem(block, 2))):
                at = (2 * k + j) * tiles * tile
                seen = (ints[at : at + 1] == seg_q) & ((first - 2 * k) * rows + lane <= row_pos)
                at = prefix_keys + (2 * k + j) * rows
                bias_ref[:, at : at + rows] = jnp.where(seen, 0.0, FILL)

    if fresh:
        pl.when(pl.program_id(0) == 0)(masks)

    def body(near):
        each = step // span
        steps = prefix_keys // step + near + 1

        def score(slab):
            head = pl.ds(slab // (GQ // SLAB) * HD, HD)
            of = range(slab * SLAB, (slab + 1) * SLAB)
            q = jnp.concatenate([q_ref[:, g * HD : (g + 1) * HD] for g in of])
            refs_of = [pk_refs[at : at + each] for at in range(0, parts, each)]
            refs_of += [k_refs[2 * k : 2 * k + 2] for k in range(near + 1)]
            top = None
            for i in range(steps):
                at = slice(i * step, (i + 1) * step)
                keys = jnp.concatenate([ref[:, head] for ref in refs_of[i]])
                s = lax.dot_general(q, keys, nt, preferred_element_type=jnp.float32)
                s = (s.reshape(SLAB, rows, step) + bias_ref[:, at][None]).reshape(-1, step)
                s_ref[slab % 2, :, at] = s
                high = jnp.maximum(s[:, :rows], s[:, rows:])
                top = high if top is None else jnp.maximum(top, high)
            top = jnp.max(top, axis=1, keepdims=True)
            top_ref[slab % 2] = jnp.broadcast_to(top, (SLAB * rows, HD))

        def weigh(slab):
            head = pl.ds(slab // (GQ // SLAB) * HD, HD)
            values = [ref[:, head] for ref in (*pv_refs, *v_refs[: 2 * near + 2])]
            values = jnp.concatenate(values)
            values = jnp.concatenate([values, jnp.ones_like(values)], axis=1)
            top = top_ref[slab % 2]
            weights = [
                jnp.exp2((s_ref[slab % 2, :, i * HD : (i + 1) * HD] - top) * scale).astype(
                    jnp.bfloat16
                )
                for i in range(steps * step // HD)
            ]
            acc = jnp.dot(
                jnp.concatenate(weights, axis=1), values, preferred_element_type=jnp.float32
            )
            out = (acc[:, :HD] / acc[:, HD:]).astype(o_ref.dtype)
            for j in range(SLAB):
                g = slab * SLAB + j
                o_ref[:, g * HD : (g + 1) * HD] = out[j * rows : (j + 1) * rows]

        slabs = BOTH * GQ // SLAB
        score(0)
        for slab in range(slabs):
            if slab + 1 < slabs:
                score(slab + 1)
            weigh(slab)

    for near in range(pairs):
        pl.when(reach_ref[0] == near)(functools.partial(body, near))


def attend(meta, queries, pieces, prefix, tile, tiles, segments=None, before=None):
    rows = queries.shape[0]
    span = prefix[0].shape[0]
    pairs, parts = len(pieces) // 2, len(prefix)
    pieces, places = zip(*[piece if isinstance(piece, tuple) else (piece, 0) for piece in pieces])
    heads = pieces[0].shape[1] // (2 * HD)
    blocks = heads // BOTH
    keys = rows * len(pieces) + span * parts
    whole = pl.BlockSpec((rows, keys), lambda i, m: (0, 0))
    scalar = pl.BlockSpec(memory_space=pltpu.SMEM)
    wide = pl.BlockSpec((rows, BOTH * GQ * HD), lambda i, m: (0, m[1] + i))
    fresh = before is None
    queries, *pieces = [
        pltpu.with_memory_space_constraint(array, pltpu.HBM) for array in (queries, *pieces)
    ]
    args = [meta, *([segments, *prefix] if fresh else before[1:])]
    args += [queries, *prefix, *prefix, *pieces, *pieces]
    if fresh:
        ints = pl.BlockSpec((span, rows), lambda i, m: (0, 2 * KVH))
        in_specs = [pl.BlockSpec((1, rows), lambda i, m: (0, 0)), *[ints] * parts]
    else:
        in_specs = [whole, scalar]
    in_specs += [
        wide,
        *[pl.BlockSpec((span, BOTH * HD), lambda i, m: (0, m[1] + i))] * parts,
        *[pl.BlockSpec((span, BOTH * HD), lambda i, m: (0, KVH // BOTH + m[1] + i))] * parts,
        *[pl.BlockSpec((rows, BOTH * HD), lambda i, m, at=at: (at, i)) for at in places],
        *[pl.BlockSpec((rows, BOTH * HD), lambda i, m, at=at: (at, blocks + i)) for at in places],
    ]
    out_specs = [wide]
    out_shape = [jax.ShapeDtypeStruct(queries.shape, queries.dtype)]
    aliases = {}
    if fresh:
        out_specs += [whole, scalar]
        out_shape += [
            jax.ShapeDtypeStruct((rows, keys), jnp.float32),
            jax.ShapeDtypeStruct((1,), jnp.int32),
        ]
    else:
        args.append(before[0])
        in_specs.append(pl.BlockSpec(memory_space=pl.ANY))
        aliases = {len(args) - 1: 0}
    return pl.pallas_call(
        functools.partial(attend_kernel, pairs, parts, tile, tiles, fresh),
        grid_spec=pltpu.PrefetchScalarGridSpec(
            num_scalar_prefetch=1,
            grid=(blocks,),
            in_specs=in_specs,
            out_specs=out_specs,
            scratch_shapes=[
                pltpu.VMEM((2, SLAB * rows, keys), jnp.float32),
                pltpu.VMEM((2, SLAB * rows, HD), jnp.float32),
            ],
        ),
        out_shape=out_shape,
        input_output_aliases=aliases,
        compiler_params=pltpu.CompilerParams(vmem_limit_bytes=32 * 1024 * 1024),
    )(*args)


def on_device(queries, resp_kv, resp_segments, prefix_kv, tile_plan, prompt_lengths):
    rows = queries.shape[1]
    tiles, tile, columns = prefix_kv.shape
    groups, count = lax.axis_size("prompt"), lax.axis_size("resp")
    group = lax.axis_index("prompt")
    block = lax.axis_index("resp")
    side = block % 2
    steps = min(count // 2 - 1, (REACH + 1) // 2)
    assert tiles == groups

    def swap(value, first):
        return lax.ppermute(value, "resp", [(r, r ^ 1) for r in range(2 * first, count)])

    def climb(value, step):
        pairs = [(r, r + 2) for r in range(2 * step - 2, count - 2)]
        return lax.ppermute(value, "resp", pairs)

    def shift(value, axis, by):
        size = lax.axis_size(axis)
        return lax.ppermute(value, axis, [(r, (r + by) % size) for r in range(size)])

    def after(value, *others):
        return lax.optimization_barrier((value, *others))[0]

    mine, theirs = halves(resp_kv[0], side)
    partner = swap(theirs, 0)
    upper = [(r, r + 1) for r in range(0, count, 2)]
    upper = lax.ppermute(after(mine, partner), "resp", upper)
    straight, crossed = [mine, partner], [theirs, upper]
    for step in range(1, steps + 1):
        one, two = straight[-2:]
        if step > 2:
            one, two = after(one, crossed[-3]), after(two, crossed[-4], upper)
        one, two = climb(one, step), climb(two, step)
        straight += [one, two]
        crossed += [swap(two, step), swap(one, step)]

    owners = (group + jnp.arange(groups, dtype=jnp.int32)) % groups
    pick = tile_plan[None, :, 0] == owners[:, None]
    place = jnp.sum(jnp.where(pick, tile_plan[None, :, 1], 0), axis=1, dtype=jnp.int32)
    own_tiles = jnp.sum(
        jnp.where(pick[:, :, None, None], prefix_kv[None], 0).astype(jnp.float32), axis=1
    )
    row = jnp.arange(tile, dtype=jnp.int32)[:, None]
    extra = jnp.where(row == 0, resp_segments[0], place.reshape(groups, 1, 1))
    own_tiles = jnp.concatenate([own_tiles, extra.astype(jnp.float32)], axis=-1)
    own_tiles = own_tiles.astype(prefix_kv.dtype)
    came = [own_tiles[0]] + [shift(own_tiles[by], "prompt", by) for by in range(1, groups)]
    came = jnp.concatenate(came)
    prefix = [jnp.concatenate([came, swap(came, 0)])]
    behind = [(), (crossed[5], straight[5]), (straight[6],)]
    for by in range(1, count // 2):
        source = after(prefix[0], *behind[min(by, len(behind)) - 1])
        prefix.append(shift(source, "resp", 2 * by))

    def meta(first):
        return jnp.stack([block, first * (KVH // 2 // BOTH), prompt_lengths[0]])

    done = attend(
        meta(side), queries[0], straight, prefix, tile, tiles, segments=resp_segments
    )
    done = attend(meta(1 - side), queries[0], crossed, prefix, tile, tiles, before=done)
    return done[0][None]


def solution(mesh):
    return jax.shard_map(
        on_device,
        mesh=mesh,
        in_specs=(
            P("prompt", "resp", None),
            P("prompt", "resp", None),
            P("prompt", "resp"),
            P(("prompt", "resp"), None, None),
            P(("prompt", "resp"), None),
            P("prompt"),
        ),
        out_specs=P("prompt", "resp", None),
        check_vma=False,
    )
```
